32 devices in a mesh: ep: 8 (over z, y), dp: 4 (over x, core).
Axes of the slice: x: 2, y: 2, z: 4, core: 2. Of those that a mesh axis runs over, the one named last changes fastest.
Arguments:
- tokens: bfloat16 [4, 32, 3584], P(None, ('ep', 'dp')), may hold values from -6 to 6
- route_weight: bfloat16 [4, 32, 2], P(None, ('ep', 'dp')), may hold values from 0.049804688 to 0.5
- expert_ids: int32 [4, 32, 2], P(None, ('ep', 'dp')), may hold values from 0 to 3, all different within a row; in each aligned block of 4 rows (0 to 3, 4 to 7, ..., all dimensions but the last counted through in order) at most 4 rows name the same one
- replica: int32 [4, 32, 2], P(None, ('ep', 'dp')), may hold values from 0 to 1
- placement: int32 [4, 2], replicated, may hold values from 0 to 3, as said below
- w_gate: bfloat16 [8, 3584, 512], P('ep', None, 'dp'), as said below
- w_up: bfloat16 [8, 3584, 512], P('ep', None, 'dp'), as said below
- w_down: bfloat16 [8, 512, 3584], P('ep', 'dp'), as said below
Outputs:
- moe_out: bfloat16 [4, 32, 3584], P(None, ('ep', 'dp'))
- slot_rows: int32 [4, 8], P(None, 'ep')
The draws below stay inside these ranges and needn't reach their ends.
Inputs may be any that keep to these rules, and one draw needn't show every extreme that they name: `expert_ids`: in each aligned block of 4 rows (the tokens of one ep index at one step), no expert is named by more than 4 tokens; in some blocks one expert is named by exactly 4. `placement`: every slot holds exactly one expert; 0 experts have two different slots, the others have the same slot in both columns. `w_gate`: two slots of one expert hold equal weights. `w_up`: two slots of one expert hold equal weights. `w_down`: two slots of one expert hold equal weights.
All inputs are finite; a program needn't handle non-finite values.
Results may differ from the reference program's by a relative error of at most 0.0059.
Values may be sent and summed in bfloat16 or wider, within the bound.
A program may use at most 128 MiB of HBM per device.

```python
import math
import jax
import jax.numpy as jnp
import numpy as np
from jax import lax

D = 3584
FF = 1024
STEPS = 4
SLOTS = 4
REDUNDANT = 0
LOGICAL = 4
TOP = 2
GROUP = 4
CAP = 4
HID = 128
TOKENS = 32
N_EP = 8
N_DP = 4


def plan_slots(key):
    shuffled = jax.random.permutation(key, SLOTS).astype(jnp.int32)
    copied = jax.random.permutation(jax.random.fold_in(key, 1), LOGICAL)[:REDUNDANT].astype(jnp.int32)
    primary = shuffled[:LOGICAL]
    second = primary.at[copied].set(shuffled[LOGICAL:])
    owners = jnp.zeros((SLOTS,), jnp.int32).at[primary].set(jnp.arange(LOGICAL, dtype=jnp.int32))
    owners = owners.at[shuffled[LOGICAL:]].set(copied)
    return (primary, second, owners)


def expert_matrix(key, owners, row_count, column_count, factor):

    def one_device(device):
        expert_key = jax.random.fold_in(jax.random.fold_in(key, owners[device // 2]), device % 2)
        return jax.random.normal(expert_key, (row_count, column_count), jnp.float32) * factor
    return jax.vmap(one_device)(jnp.arange(N_EP, dtype=jnp.int32))


def draw_placement(key, part):
    primary, second, owners = plan_slots(key)
    return jnp.stack([primary, second], axis=1).astype(jnp.int32)


def draw_w_gate(key, part):
    owners = plan_slots(key)[2]
    key = jax.random.fold_in(key, 11)
    return expert_matrix(key, owners, D, FF // 2, D ** (-0.5)).astype(jnp.bfloat16)


def draw_w_up(key, part):
    owners = plan_slots(key)[2]
    key = jax.random.fold_in(key, 12)
    return expert_matrix(key, owners, D, FF // 2, D ** (-0.5)).astype(jnp.bfloat16)


def draw_w_down(key, part):
    owners = plan_slots(key)[2]
    key = jax.random.fold_in(key, 13)
    return expert_matrix(key, owners, FF // 2, D, FF ** (-0.5)).astype(jnp.bfloat16)


def plant(values, own_key, least, top_value):
    index_at = [jax.random.randint(jax.random.fold_in(own_key, axis), (), 0, length) for axis, length in enumerate(values.shape)]
    longest = values.shape.index(max(values.shape))
    next_to = index_at[:longest] + [(index_at[longest] + 1) % values.shape[longest]] + index_at[longest + 1:]
    return values.at[tuple(index_at)].set(least).at[tuple(next_to)].set(top_value)


def block_scale(key, shape, shards, least, top_value):
    def one(dim, shards_of):
        heights = jax.random.uniform(jax.random.fold_in(jax.random.fold_in(key, 6), dim), (shards_of,), jnp.float32, least / len(shards), top_value / len(shards))
        return jnp.repeat(jnp.exp(heights), shape[dim] // shards_of).reshape((-1,) + (1,) * (len(shape) - dim - 1))

    factor_of = one(*shards[0])
    for cut in shards[1:]:
        factor_of = factor_of * one(*cut)
    return factor_of


def assign_block(own_key, own, number, rows, amount, top, limit, lean):
    ranking = jax.random.permutation(own_key, amount)
    packed, common = portions_of(amount, rows * top, limit, lean, True), portions_of(amount, rows * top, limit, lean, False)
    places = jnp.arange(amount)

    def named(lengths, turn):
        used = int((lengths > 0).sum())
        fixed = max(1, used // 4)
        passed = fixed + (places - fixed + turn * (used - fixed)) % max(1, amount - fixed)
        return jnp.zeros((amount,), jnp.int32).at[ranking[jnp.where(places < fixed, places, passed)]].set(jnp.asarray(lengths, jnp.int32))

    lengths = jnp.where(number % 4 == 0, named(packed, number // 4), named(common, number - number // 4 - 1))
    mixed = jax.random.permutation(jax.random.fold_in(own, 3), amount)
    source_of, taker = mixed[0:amount // 2 * 2:2], mixed[1:amount // 2 * 2:2]
    room = jnp.minimum(lengths[source_of] - 1, limit - lengths[taker]) // 2
    room = jnp.where((source_of == ranking[0]) | (taker == ranking[0]) | (lengths[taker] == 0), 0, jnp.maximum(room, 0))
    passed = jax.random.randint(jax.random.fold_in(own, 4), (amount // 2,), 0, 1 << 20) % (room + 1)
    lengths = lengths.at[source_of].add(-passed).at[taker].add(passed)
    labels = jnp.searchsorted(jnp.cumsum(lengths), jnp.arange(rows * top), side="right").astype(jnp.int32)
    grid = labels.reshape(top, rows).T
    grid = grid[jax.random.permutation(jax.random.fold_in(own, 1), rows)]
    turn = jax.random.randint(jax.random.fold_in(own, 2), (rows, 1), 0, top)
    return jnp.take_along_axis(grid, (jnp.arange(top)[None, :] + turn) % top, axis=1)


def portions_of(amount, total, reach, slope, full):
    weights = [(1 << 20) // math.isqrt(rank ** slope) + 1 for rank in range(1, amount + 1)]
    largest = reach if full else min(reach, max(-(-total // amount), total * weights[0] // sum(weights)))
    least = 1 if total - largest >= amount - 1 else 0
    holding, spare = [largest] + [least] * (amount - 1), total - largest - least * (amount - 1)
    while spare > 0:
        candidates = [i for i in range(1, amount) if holding[i] < largest] or [i for i in range(1, amount) if holding[i] < reach]
        whole, left = sum([weights[i] for i in candidates]), spare
        for i in candidates:
            more = min(reach - holding[i], max(1, left * weights[i] // whole), spare)
            holding[i] = holding[i] + more
            spare = spare - more
    return np.array(holding)


def centred(rng, shape, width, limit, cuts=(), held_as=jnp.bfloat16):
    gain = block_scale(rng, shape, cuts, -0.22, 0.18) if cuts else 1.0
    entries = jax.random.normal(rng, shape, jnp.float32) * width * gain
    return jnp.minimum(jnp.maximum(entries, -limit), limit).astype(held_as)


def setup_inputs(seed: int = 0) -> dict:
    splits = jax.random.split(jax.random.key(seed), 9)
    tokens = centred(splits[0], (STEPS, TOKENS, D), 1.0, 6.0, ((1, 32),))
    route_weight = jnp.clip(jnp.exp(math.log(0.5) - 2.306499 * jax.random.uniform(splits[1], (STEPS, TOKENS, TOP), jnp.float32) ** block_scale(splits[1], (STEPS, TOKENS, TOP), ((1, 32),), -0.2, 0.2)), 0.049804688, 0.5).astype(jnp.bfloat16)
    expert_ids_keys = jax.random.split(jax.random.fold_in(splits[2], 1), STEPS * TOKENS // GROUP)
    expert_ids_turns = jax.random.permutation(jax.random.fold_in(splits[2], 3), STEPS * TOKENS // GROUP)
    expert_ids = jax.vmap(lambda own, number: assign_block(jax.random.fold_in(splits[2], 2), own, number, GROUP, LOGICAL, TOP, CAP, 2))(expert_ids_keys, expert_ids_turns).reshape((STEPS, TOKENS, TOP))
    replica = plant(jax.random.randint(splits[3], (STEPS, TOKENS, TOP), 0, 2), jax.random.fold_in(splits[3], 1), 0, 1).astype(jnp.int32)
    placement = draw_placement(jax.random.fold_in(splits[8], 71), 0)
    w_gate = draw_w_gate(jax.random.fold_in(splits[8], 71), 0)
    w_up = draw_w_up(jax.random.fold_in(splits[8], 71), 0)
    w_down = draw_w_down(jax.random.fold_in(splits[8], 71), 0)
    return {"tokens": tokens, "route_weight": route_weight, "expert_ids": expert_ids, "replica": replica, "placement": placement, "w_gate": w_gate, "w_up": w_up, "w_down": w_down}


def pick_slots(expert_ids, replica, placement):
    logical = placement.shape[0]
    chosen = jnp.where(replica[..., None] == 0, placement[:, 0], placement[:, 1])
    matches = expert_ids[..., None] == jnp.arange(logical, dtype=jnp.int32)
    return jnp.sum(jnp.where(matches, chosen, 0), axis=-1).astype(jnp.int32)


def place_rows(group_slots, slot_count):
    flat_slots = group_slots.reshape(-1)
    matches = (flat_slots[:, None] == jnp.arange(slot_count, dtype=jnp.int32)[None, :]).astype(jnp.int32)
    earlier = (jnp.cumsum(matches, axis=0) - matches).astype(jnp.int32)
    position = jnp.sum(earlier * matches, axis=1).astype(jnp.int32)
    counts = jnp.sum(matches, axis=0).astype(jnp.int32)
    return position.reshape(group_slots.shape), counts


def expert_pair(expert_rows, gate_pair, up_pair, down_pair):
    running = jnp.zeros((expert_rows.shape[0], down_pair.shape[2]), jnp.float32)
    for half_index in range(2):
        gate_out = jnp.dot(expert_rows, gate_pair[half_index], preferred_element_type=jnp.float32)
        up_out = jnp.dot(expert_rows, up_pair[half_index], preferred_element_type=jnp.float32)
        hidden = (jax.nn.silu(gate_out) * up_out).astype(jnp.bfloat16)
        for block_index in range(N_DP):
            block_start = block_index * HID
            block_out = jnp.dot(hidden[:, block_start:block_start + HID], down_pair[half_index, block_start:block_start + HID], preferred_element_type=jnp.float32).astype(jnp.bfloat16)
            running = running + block_out.astype(jnp.float32)
    return running


def reference(tokens, route_weight, expert_ids, replica, placement, w_gate, w_up, w_down):
    slot_table = pick_slots(expert_ids, replica, placement)
    group_index = jnp.arange(N_EP, dtype=jnp.int32)[:, None, None]
    outputs = []
    load_rows = []
    for step_index in range(STEPS):
        grouped = tokens[step_index].reshape(N_EP, GROUP, D)
        group_slots = slot_table[step_index].reshape(N_EP, GROUP, TOP)
        position, counts = jax.vmap(lambda one_group: place_rows(one_group, SLOTS))(group_slots)
        source = jnp.broadcast_to(grouped[:, :, None, :], (N_EP, GROUP, TOP, D))
        buffer = jnp.zeros((SLOTS, N_EP, CAP, D), tokens.dtype).at[group_slots, group_index, position].set(source)

        def per_slot(slot_index):
            gate_pair = lax.dynamic_slice_in_dim(w_gate, 2 * slot_index, 2, 0)
            up_pair = lax.dynamic_slice_in_dim(w_up, 2 * slot_index, 2, 0)
            down_pair = lax.dynamic_slice_in_dim(w_down, 2 * slot_index, 2, 0)
            expert_rows = lax.dynamic_index_in_dim(buffer, slot_index, 0, keepdims=False).reshape(N_EP * CAP, D)
            return expert_pair(expert_rows, gate_pair, up_pair, down_pair).reshape(N_EP, CAP, D)

        expert_out = lax.map(per_slot, jnp.arange(SLOTS, dtype=jnp.int32))
        picked = expert_out[group_slots, group_index, position]
        weights = route_weight[step_index].reshape(N_EP, GROUP, TOP).astype(jnp.float32)
        combined = jnp.sum(picked * weights[..., None], axis=2)
        outputs.append(combined.reshape(TOKENS, D).astype(jnp.bfloat16))
        load_rows.append(jnp.repeat(jnp.sum(counts, axis=0), 2).astype(jnp.int32))
    return jnp.stack(outputs), jnp.stack(load_rows)
```

```python
import functools

import jax
import jax.numpy as jnp
from jax import lax
from jax.experimental import pallas as pl
from jax.experimental.pallas import tpu as pltpu
from jax.sharding import PartitionSpec as P

MESH = pl.DeviceIdType.MESH
LANES = 128


def pick_slots(expert_ids, replica, placement):
    logical = placement.shape[0]
    chosen = jnp.where(replica[..., None] == 0, placement[:, 0], placement[:, 1])
    matches = expert_ids[..., None] == jnp.arange(logical, dtype=jnp.int32)
    return jnp.sum(jnp.where(matches, chosen, 0), axis=-1)


def place_rows(group_slots, slot_count):
    flat_slots = group_slots.reshape(-1)
    matches = (flat_slots[:, None] == jnp.arange(slot_count, dtype=jnp.int32)[None, :]).astype(
        jnp.int32
    )
    earlier = jnp.cumsum(matches, axis=0) - matches
    position = jnp.sum(earlier * matches, axis=1)
    counts = jnp.sum(matches, axis=0)
    return (position.reshape(group_slots.shape), counts)


def pack_rows(rows, slots, slot_count, capacity, top_count):
    position, counts = place_rows(slots, slot_count)
    target = (slots * capacity + position).reshape(-1)
    repeated = jnp.repeat(rows, top_count, axis=0)
    packed = jnp.zeros((slot_count * capacity, rows.shape[1]), rows.dtype).at[target].set(repeated)
    return (packed.reshape(slot_count, capacity, rows.shape[1]), target)


def expert_block(expert_rows, w_gate, w_up, w_down):
    gate_out = jnp.dot(expert_rows, w_gate[0], preferred_element_type=jnp.float32)
    up_out = jnp.dot(expert_rows, w_up[0], preferred_element_type=jnp.float32)
    hidden = (jax.nn.silu(gate_out) * up_out).astype(jnp.bfloat16)
    return jnp.dot(hidden, w_down[0], preferred_element_type=jnp.float32).astype(jnp.bfloat16)


def combine_rows(
    returned, target, weight_rows, row_count, top_count, slot_count, capacity, model_width
):
    paired = returned.reshape(slot_count, 2, capacity, model_width)
    first_half = paired[:, 0].reshape(-1, model_width)[target].astype(jnp.float32)
    second_half = paired[:, 1].reshape(-1, model_width)[target].astype(jnp.float32)
    weighted = (first_half + second_half) * weight_rows.reshape(-1, 1).astype(jnp.float32)
    return jnp.sum(weighted.reshape(row_count, top_count, model_width), axis=1)


def local_packed(tokens, route_weight, expert_ids, replica, placement, w_gate, w_up, w_down):
    steps_total = tokens.shape[0]
    model_width = tokens.shape[2]
    ep_count = lax.axis_size("ep")
    dp_count = lax.axis_size("dp")
    slot_count = ep_count // 2
    logical = placement.shape[0]
    top_count = expert_ids.shape[2]
    own_count = expert_ids.shape[1]
    group_size = own_count * dp_count
    capacity = 2 * ((group_size * top_count + logical) // (2 * logical)) + 2
    own_slots = pick_slots(expert_ids, replica, placement)
    outputs = []
    load_rows = []
    for step_index in range(steps_total):
        group_slots = lax.all_gather(own_slots[step_index], "dp", axis=0, tiled=True)
        group_counts = place_rows(group_slots, slot_count)[1]
        arrived_counts = lax.all_to_all(
            jnp.repeat(group_counts, 2), "ep", split_axis=0, concat_axis=0, tiled=True
        )
        grouped, group_weight = (
            lax.all_gather(tokens[step_index], "dp", axis=0, tiled=True),
            lax.all_gather(route_weight[step_index], "dp", axis=0, tiled=True),
        )
        send_rows, target = pack_rows(grouped, group_slots, slot_count, capacity, top_count)
        arrived = lax.all_to_all(
            jnp.repeat(send_rows, 2, axis=0), "ep", split_axis=0, concat_axis=0, tiled=True
        )
        block_out = expert_block(arrived.reshape(-1, model_width), w_gate, w_up, w_down)
        returned = lax.all_to_all(
            block_out.reshape(ep_count, capacity, model_width),
            "ep",
            split_axis=0,
            concat_axis=0,
            tiled=True,
        )
        partial_tokens = combine_rows(
            returned, target, group_weight, group_size, top_count, slot_count, capacity, model_width
        )
        token_out = lax.psum_scatter(partial_tokens, "dp", scatter_dimension=0, tiled=True)
        outputs.append(token_out.astype(jnp.bfloat16))
        load_rows.append(jnp.sum(arrived_counts).reshape(1))
    return (jnp.stack(outputs), jnp.stack(load_rows))


def moe_kernel(
    steps,
    msg_ref,
    w_gate_ref,
    w_up_ref,
    w_down_ref,
    out_ref,
    count_ref,
    wgu,
    wd,
    zbuf,
    gx,
    ps,
    cs,
    cr,
    first_s,
    second_s,
    first_r,
    second_r,
    tbuf,
    zr,
    wsem,
    ssem,
    rsem,
):
    ep, dp = lax.axis_index("ep"), lax.axis_index("dp")
    z, y = ep // 2, ep % 2
    x, c = dp // 2, dp % 2
    width = wgu.shape[0]
    cols = width // LANES
    rows_own = cols * steps
    hid = w_gate_ref.shape[2]
    f32, bf16 = jnp.float32, jnp.bfloat16

    loads = [
        pltpu.make_async_copy(w_gate_ref.at[0], wgu.at[:, pl.ds(0, hid)], wsem.at[0]),
        pltpu.make_async_copy(w_up_ref.at[0], wgu.at[:, pl.ds(hid, hid)], wsem.at[1]),
        pltpu.make_async_copy(w_down_ref.at[0], wd, wsem.at[2]),
    ]
    for load in loads:
        load.start()

    def device(zz, yy, xx, cc):
        return (zz * 2 + yy, xx * 2 + cc)

    z_others = [z + 1 - 2 * (z % 2), (z + 2) % 4, 3 - z]
    z_dev = [device(zz, y, x, c) for zz in z_others]
    core_dev = device(z, y, x, 1 - c)
    first_dev = device(z, y + c * (1 - 2 * y), x + (1 - c) * (1 - 2 * x), c)
    second_dev = device(z, y + (1 - c) * (1 - 2 * y), x + c * (1 - 2 * x), c)
    slot_a, slot_b = 2 - c, 1 + c

    barrier = pltpu.get_barrier_semaphore()
    partners = z_dev + [core_dev, first_dev, second_dev]
    for partner in partners:
        pl.semaphore_signal(barrier, inc=1, device_id=partner, device_id_type=MESH)
    pl.semaphore_wait(barrier, len(partners))

    started = []

    def send(src, dst, to):
        n = len(started)
        copy = pltpu.make_async_remote_copy(
            src_ref=src,
            dst_ref=dst,
            send_sem=ssem.at[n],
            recv_sem=rsem.at[n],
            device_id=to,
            device_id_type=MESH,
        )
        copy.start()
        started.append(copy)
        return copy

    z_in = [send(msg_ref, zbuf.at[k + 1], z_dev[k]) for k in (2, 1, 0)]
    zbuf[0] = msg_ref[...]
    per = zbuf.shape[1]
    block = 4 * steps
    r = lax.broadcasted_iota(jnp.int32, ((cols + 1) * block, 4 * per), 0)
    q = lax.broadcasted_iota(jnp.int32, ((cols + 1) * block, 4 * per), 1)
    source = (r % block) // steps * per + r // block * steps + r % steps
    spread = jnp.where(source == q, 1.0, 0.0).astype(bf16)
    for copy in z_in:
        copy.wait_recv()
    mixed = jnp.dot(spread, zbuf[...].reshape(4 * per, LANES), preferred_element_type=f32)
    mixed = mixed.astype(bf16)
    for j in range(cols + 1):
        gx[0, :, j * LANES : (j + 1) * LANES] = mixed[j * block : (j + 1) * block]

    own_a = send(gx.at[0], gx.at[slot_a], first_dev)
    own_b = send(gx.at[0], gx.at[slot_b], second_dev)
    from_core = [send(gx.at[0], gx.at[4], core_dev)]
    own_a.wait_recv()
    diag = send(gx.at[slot_a], gx.at[3], second_dev)
    from_core.append(send(gx.at[slot_a], gx.at[4 + slot_a], core_dev))
    own_b.wait_recv()
    from_core.append(send(gx.at[slot_b], gx.at[4 + slot_b], core_dev))
    diag.wait_recv()
    from_core.append(send(gx.at[3], gx.at[7], core_dev))
    for load in loads:
        load.wait()
    for copy in from_core:
        copy.wait_recv()

    total = 8 * block
    tokens = gx[:, :, 0:width].reshape(total, width)
    both = jnp.dot(tokens, wgu[...], preferred_element_type=f32)
    gate, up = both[:, :hid], both[:, hid:]
    hidden = (gate / (1.0 + jnp.exp(-gate)) * up).astype(bf16)
    route = gx[:, :, width : width + LANES].reshape(total, LANES).astype(f32)
    lane = lax.broadcasted_iota(jnp.int32, (total, LANES), 1)
    weight = jnp.sum(jnp.where(lane == z, route, 0.0), axis=1, keepdims=True)
    counted = jnp.sum(jnp.where(lane == z + 4, route, 0.0), axis=1, keepdims=True)
    row = lax.broadcasted_iota(jnp.int32, (total, LANES), 0)
    per_step = jnp.where(lane == row % steps, counted, 0.0)
    count_ref[...] = jnp.sum(per_step, axis=0, keepdims=True).astype(jnp.int32)

    half = total // 2
    theirs = jnp.dot(hidden[half:], wd[...], preferred_element_type=f32) * weight[half:]
    cs[...] = theirs.astype(bf16).reshape(4, block, width)
    to_core = send(cs, cr, core_dev)
    mine = jnp.dot(hidden[:half], wd[...], preferred_element_type=f32) * weight[:half]
    ps[...] = mine.reshape(4, block, width)
    to_core.wait_recv()

    first_s[0] = (ps[3] + cr[3].astype(f32)).astype(bf16)
    diag_out = send(first_s.at[0], first_r.at[0], first_dev)
    first_s[1] = (ps[slot_a] + cr[slot_a].astype(f32)).astype(bf16)
    first_out = send(first_s.at[1], first_r.at[1], first_dev)
    held = ps[slot_b] + cr[slot_b].astype(f32)
    diag_out.wait_recv()
    second_s[...] = (held + first_r[0].astype(f32)).astype(bf16)
    second_out = send(second_s, second_r, second_dev)
    held = ps[0] + cr[0].astype(f32)
    first_out.wait_recv()
    held = held + first_r[1].astype(f32)
    r = lax.broadcasted_iota(jnp.int32, (4 * rows_own, cols * block), 0)
    q = lax.broadcasted_iota(jnp.int32, (4 * rows_own, cols * block), 1)
    source = (r % rows_own) // steps * block + r // rows_own * steps + r % steps
    gather = jnp.where(source == q, 1.0, 0.0).astype(bf16)
    second_out.wait_recv()
    summed = (held + second_r[...].astype(f32)).astype(bf16)
    stacked = jnp.concatenate(
        [summed[:, j * LANES : (j + 1) * LANES] for j in range(cols)], axis=0
    )
    split = jnp.dot(gather, stacked, preferred_element_type=f32)
    tbuf[...] = split.astype(bf16).reshape(4, rows_own, LANES)
    z_out = [send(tbuf.at[k + 1], zr.at[k], z_dev[k]) for k in (2, 1, 0)]
    final = tbuf[0].astype(f32)
    for copy in z_out:
        copy.wait_recv()
    for k in range(3):
        final = final + zr[k].astype(f32)
    out_ref[...] = final
    for copy in started:
        copy.wait_send()


def local_gathered(tokens, route_weight, expert_ids, replica, placement, w_gate, w_up, w_down):
    steps, own, width = tokens.shape
    hid = w_gate.shape[2]
    cols = width // LANES
    slots = pick_slots(expert_ids, replica, placement)[:, 0, :]
    hits = slots[:, :, None] == jnp.arange(4, dtype=jnp.int32)
    weights = jnp.sum(jnp.where(hits, route_weight[:, 0, :, None].astype(jnp.float32), 0.0), axis=1)
    counts = jnp.sum(hits.astype(jnp.float32), axis=1)
    extra = jnp.concatenate([weights, counts], axis=1).astype(jnp.bfloat16)
    extra = jnp.pad(extra, ((0, 16 - steps), (0, LANES - 8)))
    rows = tokens.reshape(steps, cols, LANES).transpose(1, 0, 2).reshape(cols * steps, LANES)
    message = jnp.concatenate([rows, extra], axis=0)
    per = message.shape[0]
    block = 4 * steps
    bf16 = jnp.bfloat16
    vmem = pl.BlockSpec(memory_space=pltpu.VMEM)
    anywhere = pl.BlockSpec(memory_space=pl.ANY)
    out, count = pl.pallas_call(
        functools.partial(moe_kernel, steps),
        out_shape=(
            jax.ShapeDtypeStruct((cols * steps, LANES), jnp.float32),
            jax.ShapeDtypeStruct((1, LANES), jnp.int32),
        ),
        in_specs=[vmem, anywhere, anywhere, anywhere],
        out_specs=(vmem, vmem),
        scratch_shapes=[
            pltpu.VMEM((width, 2 * hid), bf16),
            pltpu.VMEM((hid, width), bf16),
            pltpu.VMEM((4, per, LANES), bf16),
            pltpu.VMEM((8, block, width + LANES), bf16),
            pltpu.VMEM((4, block, width), jnp.float32),
            pltpu.VMEM((4, block, width), bf16),
            pltpu.VMEM((4, block, width), bf16),
            pltpu.VMEM((2, block, width), bf16),
            pltpu.VMEM((block, width), bf16),
            pltpu.VMEM((2, block, width), bf16),
            pltpu.VMEM((block, width), bf16),
            pltpu.VMEM((4, cols * steps, LANES), bf16),
            pltpu.VMEM((3, cols * steps, LANES), bf16),
            pltpu.SemaphoreType.DMA((3,)),
            pltpu.SemaphoreType.DMA((18,)),
            pltpu.SemaphoreType.DMA((18,)),
        ],
        compiler_params=pltpu.CompilerParams(
            collective_id=0, has_side_effects=True, vmem_limit_bytes=48 * 1024 * 1024
        ),
    )(message, w_gate, w_up, w_down)
    moe = out.reshape(cols, steps, LANES).transpose(1, 0, 2).reshape(steps, own, width)
    return moe.astype(jnp.bfloat16), count[0, :steps].reshape(steps, 1)


def solution(mesh):
    dense = mesh.shape["ep"] == 8 and mesh.shape["dp"] == 4
    return jax.shard_map(
        local_gathered if dense else local_packed,
        mesh=mesh,
        in_specs=(
            P(None, ("ep", "dp"), None),
            P(None, ("ep", "dp"), None),
            P(None, ("ep", "dp"), None),
            P(None, ("ep", "dp"), None),
            P(),
            P("ep", None, "dp"),
            P("ep", None, "dp"),
            P("ep", "dp", None),
        ),
        out_specs=(P(None, ("ep", "dp"), None), P(None, "ep")),
        check_vma=False,
    )
```

```python
import functools

import jax
import jax.numpy as jnp
from jax import lax
from jax.experimental import pallas as pl
from jax.experimental.pallas import tpu as pltpu
from jax.sharding import PartitionSpec as P

MESH = pl.DeviceIdType.MESH
LANES = 128
VMEM_LIMIT = 60 * 1024 * 1024


def pick_slots(expert_ids, replica, placement):
    logical = placement.shape[0]
    chosen = jnp.where(replica[..., None] == 0, placement[:, 0], placement[:, 1])
    matches = expert_ids[..., None] == jnp.arange(logical, dtype=jnp.int32)
    return jnp.sum(jnp.where(matches, chosen, 0), axis=-1)


def place_rows(group_slots, slot_count):
    flat_slots = group_slots.reshape(-1)
    matches = (flat_slots[:, None] == jnp.arange(slot_count, dtype=jnp.int32)[None, :]).astype(
        jnp.int32
    )
    earlier = jnp.cumsum(matches, axis=0) - matches
    position = jnp.sum(earlier * matches, axis=1)
    counts = jnp.sum(matches, axis=0)
    return (position.reshape(group_slots.shape), counts)


def pack_rows(rows, slots, slot_count, capacity, top_count):
    position, counts = place_rows(slots, slot_count)
    target = (slots * capacity + position).reshape(-1)
    repeated = jnp.repeat(rows, top_count, axis=0)
    packed = jnp.zeros((slot_count * capacity, rows.shape[1]), rows.dtype).at[target].set(repeated)
    return (packed.reshape(slot_count, capacity, rows.shape[1]), target)


def expert_block(expert_rows, w_gate, w_up, w_down):
    gate_out = jnp.dot(expert_rows, w_gate[0], preferred_element_type=jnp.float32)
    up_out = jnp.dot(expert_rows, w_up[0], preferred_element_type=jnp.float32)
    hidden = (jax.nn.silu(gate_out) * up_out).astype(jnp.bfloat16)
    return jnp.dot(hidden, w_down[0], preferred_element_type=jnp.float32).astype(jnp.bfloat16)


def combine_rows(
    returned, target, weight_rows, row_count, top_count, slot_count, capacity, model_width
):
    paired = returned.reshape(slot_count, 2, capacity, model_width)
    first_half = paired[:, 0].reshape(-1, model_width)[target].astype(jnp.float32)
    second_half = paired[:, 1].reshape(-1, model_width)[target].astype(jnp.float32)
    weighted = (first_half + second_half) * weight_rows.reshape(-1, 1).astype(jnp.float32)
    return jnp.sum(weighted.reshape(row_count, top_count, model_width), axis=1)


def local_packed(tokens, route_weight, expert_ids, replica, placement, w_gate, w_up, w_down):
    steps_total = tokens.shape[0]
    model_width = tokens.shape[2]
    ep_count = lax.axis_size("ep")
    dp_count = lax.axis_size("dp")
    slot_count = ep_count // 2
    logical = placement.shape[0]
    top_count = expert_ids.shape[2]
    own_count = expert_ids.shape[1]
    group_size = own_count * dp_count
    capacity = 2 * ((group_size * top_count + logical) // (2 * logical)) + 2
    own_slots = pick_slots(expert_ids, replica, placement)
    outputs = []
    load_rows = []
    for step_index in range(steps_total):
        group_slots = lax.all_gather(own_slots[step_index], "dp", axis=0, tiled=True)
        group_counts = place_rows(group_slots, slot_count)[1]
        arrived_counts = lax.all_to_all(
            jnp.repeat(group_counts, 2), "ep", split_axis=0, concat_axis=0, tiled=True
        )
        grouped, group_weight = (
            lax.all_gather(tokens[step_index], "dp", axis=0, tiled=True),
            lax.all_gather(route_weight[step_index], "dp", axis=0, tiled=True),
        )
        send_rows, target = pack_rows(grouped, group_slots, slot_count, capacity, top_count)
        arrived = lax.all_to_all(
            jnp.repeat(send_rows, 2, axis=0), "ep", split_axis=0, concat_axis=0, tiled=True
        )
        block_out = expert_block(arrived.reshape(-1, model_width), w_gate, w_up, w_down)
        returned = lax.all_to_all(
            block_out.reshape(ep_count, capacity, model_width),
            "ep",
            split_axis=0,
            concat_axis=0,
            tiled=True,
        )
        partial_tokens = combine_rows(
            returned, target, group_weight, group_size, top_count, slot_count, capacity, model_width
        )
        token_out = lax.psum_scatter(partial_tokens, "dp", scatter_dimension=0, tiled=True)
        outputs.append(token_out.astype(jnp.bfloat16))
        load_rows.append(jnp.sum(arrived_counts).reshape(1))
    return (jnp.stack(outputs), jnp.stack(load_rows))


def moe_kernel(
    chunks,
    tok_ref,
    rw_ref,
    ids_ref,
    rep_ref,
    place_ref,
    w_gate_ref,
    w_up_ref,
    w_down_ref,
    out_ref,
    count_ref,
    rw,
    ids,
    rep,
    place,
    wgu,
    wd,
    extra,
    zbuf,
    zextra,
    gx,
    ps,
    cs,
    cr,
    first_s,
    second_s,
    first_r,
    second_r,
    tbuf,
    zr,
    wsem,
    ssem,
    rsem,
):
    ep, dp = lax.axis_index("ep"), lax.axis_index("dp")
    z, y = ep // 2, ep % 2
    x, c = dp // 2, dp % 2
    steps, width = tok_ref.shape
    hid = w_gate_ref.shape[2]
    part = width // chunks
    block = 4 * steps
    total = 8 * block
    f32, bf16 = jnp.float32, jnp.bfloat16

    def columns(n, more=0):
        return pl.ds(n * part, part + more)

    def load(src, dst, n):
        copy = pltpu.make_async_copy(src, dst, wsem.at[n])
        copy.start()
        return copy

    small = [
        load(src, dst, n)
        for n, (src, dst) in enumerate(
            [(rw_ref, rw), (ids_ref, ids), (rep_ref, rep), (place_ref, place)]
        )
    ]
    own = [load(tok_ref.at[:, columns(n)], zbuf.at[n, 0], 4 + n) for n in range(chunks)]
    weights = [
        load(w_gate_ref.at[0], wgu.at[:, pl.ds(0, hid)], 4 + chunks),
        load(w_up_ref.at[0], wgu.at[:, pl.ds(hid, hid)], 5 + chunks),
        load(w_down_ref.at[0], wd, 6 + chunks),
    ]

    def device(zz, yy, xx, cc):
        return (zz * 2 + yy, xx * 2 + cc)

    z_others = [z + 1 - 2 * (z % 2), (z + 2) % 4, 3 - z]
    z_dev = [device(zz, y, x, c) for zz in z_others]
    core_dev = device(z, y, x, 1 - c)
    first_dev = device(z, y + c * (1 - 2 * y), x + (1 - c) * (1 - 2 * x), c)
    second_dev = device(z, y + (1 - c) * (1 - 2 * y), x + c * (1 - 2 * x), c)
    slot_a, slot_b = 2 - c, 1 + c

    barrier = pltpu.get_barrier_semaphore()
    partners = z_dev + [core_dev, first_dev, second_dev]
    for partner in partners:
        pl.semaphore_signal(barrier, inc=1, device_id=partner, device_id_type=MESH)
    pl.semaphore_wait(barrier, len(partners))

    started = []

    def send(src, dst, to):
        n = len(started)
        copy = pltpu.make_async_remote_copy(
            src_ref=src,
            dst_ref=dst,
            send_sem=ssem.at[n],
            recv_sem=rsem.at[n],
            device_id=to,
            device_id_type=MESH,
        )
        copy.start()
        started.append(copy)
        return copy

    z_in = [
        [send(tok_ref.at[:, columns(n)], zbuf.at[n, k + 1], z_dev[k]) for k in (2, 1, 0)]
        for n in range(chunks)
    ]

    for copy in small:
        copy.wait()
    lane = lax.broadcasted_iota(jnp.int32, (steps, LANES), 1)
    diagonal = lax.broadcasted_iota(jnp.int32, (steps, steps), 0) == lax.broadcasted_iota(
        jnp.int32, (steps, steps), 1
    )
    slots = jnp.zeros(ids.shape, jnp.int32)
    for e in range(place.shape[1]):
        chosen = jnp.where(rep[...] == 0, place[0:1, e : e + 1], place[1:2, e : e + 1])
        slots = slots + jnp.where(ids[...] == e, chosen, 0)
    packed = jnp.zeros((steps, LANES), f32)
    for k in range(ids.shape[0]):
        slot = jnp.sum(jnp.where(diagonal, slots[k : k + 1], 0), axis=1, keepdims=True)
        gain = rw[k : k + 1].astype(f32)
        gain = jnp.sum(jnp.where(diagonal, gain, 0.0), axis=1, keepdims=True)
        packed = packed + jnp.where(lane == slot, gain, 0.0)
        packed = packed + jnp.where(lane == slot + 4, 1.0, 0.0)
    extra[...] = packed.astype(bf16)
    z_in.append([send(extra, zextra.at[k + 1], z_dev[k]) for k in (2, 1, 0)])

    def span(n):
        return columns(n, LANES if n == chunks - 1 else 0)

    first_in, second_in, core_in, diag_in = {}, {}, {}, {}

    def spread(n):
        own[n].wait()
        for copy in z_in[n]:
            copy.wait_recv()
        gx[0, :, n * part : (n + 1) * part] = jnp.concatenate(
            [zbuf[n, k] for k in range(4)], axis=0
        )
        if n == chunks - 1:
            for copy in z_in[chunks]:
                copy.wait_recv()
            gx[0, :, width : width + LANES] = jnp.concatenate(
                [extra[...]] + [zextra[k] for k in range(1, 4)], axis=0
            )
        here = gx.at[0, :, span(n)]
        first_in[n] = send(here, gx.at[slot_a, :, span(n)], first_dev)
        second_in[n] = send(here, gx.at[slot_b, :, span(n)], second_dev)
        core_in[n] = [send(here, gx.at[4, :, span(n)], core_dev)]

    def forward(n):
        first_in[n].wait_recv()
        here = gx.at[slot_a, :, span(n)]
        diag_in[n] = send(here, gx.at[3, :, span(n)], second_dev)
        core_in[n].append(send(here, gx.at[4 + slot_a, :, span(n)], core_dev))
        second_in[n].wait_recv()
        here = gx.at[slot_b, :, span(n)]
        core_in[n].append(send(here, gx.at[4 + slot_b, :, span(n)], core_dev))

    def corner(n):
        diag_in[n].wait_recv()
        core_in[n].append(send(gx.at[3, :, span(n)], gx.at[7, :, span(n)], core_dev))

    def multiply(n, both):
        if n == 0:
            weights[0].wait()
            weights[1].wait()
        for copy in core_in[n]:
            copy.wait_recv()
        rows = gx[:, :, n * part : (n + 1) * part].reshape(total, part)
        more = jnp.dot(rows, wgu[n * part : (n + 1) * part], preferred_element_type=f32)
        return more if both is None else both + more

    both = None
    for n in range(chunks + 3):
        if n < chunks:
            spread(n)
        if 0 <= n - 1 < chunks:
            forward(n - 1)
        if 0 <= n - 2 < chunks:
            corner(n - 2)
        if 0 <= n - 3 < chunks:
            both = multiply(n - 3, both)

    gate, up = both[:, :hid], both[:, hid:]
    hidden = (gate / (1.0 + jnp.exp(-gate)) * up).astype(bf16)
    route = gx[:, :, width : width + LANES].reshape(total, LANES).astype(f32)
    lane = lax.broadcasted_iota(jnp.int32, (total, LANES), 1)
    weight = jnp.sum(jnp.where(lane == z, route, 0.0), axis=1, keepdims=True)
    weights[2].wait()

    half = total // 2
    to_core, diag_out, first_out, second_out, z_out = {}, {}, {}, {}, {}

    def down(n):
        made = jnp.dot(hidden, wd[:, n * part : (n + 1) * part], preferred_element_type=f32)
        made = made * weight
        cs[n] = made[half:].astype(bf16).reshape(4, block, part)
        to_core[n] = send(cs.at[n], cr.at[n], core_dev)
        ps[n] = made[:half].reshape(4, block, part)

    def pair(n):
        to_core[n].wait_recv()
        first_s[n, 0] = (ps[n, 3] + cr[n, 3].astype(f32)).astype(bf16)
        diag_out[n] = send(first_s.at[n, 0], first_r.at[n, 0], first_dev)
        first_s[n, 1] = (ps[n, slot_a] + cr[n, slot_a].astype(f32)).astype(bf16)
        first_out[n] = send(first_s.at[n, 1], first_r.at[n, 1], first_dev)

    def turn(n):
        held = ps[n, slot_b] + cr[n, slot_b].astype(f32)
        diag_out[n].wait_recv()
        second_s[n] = (held + first_r[n, 0].astype(f32)).astype(bf16)
        second_out[n] = send(second_s.at[n], second_r.at[n], second_dev)

    def across(n):
        held = ps[n, 0] + cr[n, 0].astype(f32)
        first_out[n].wait_recv()
        held = held + first_r[n, 1].astype(f32)
        second_out[n].wait_recv()
        held = (held + second_r[n].astype(f32)).astype(bf16)
        for k in range(4):
            tbuf[n, k] = held[k * steps : (k + 1) * steps]
        z_out[n] = [send(tbuf.at[n, k + 1], zr.at[n, k], z_dev[k]) for k in (2, 1, 0)]

    def finish(n):
        final = tbuf[n, 0].astype(f32)
        for copy in z_out[n]:
            copy.wait_recv()
        for k in range(3):
            final = final + zr[n, k].astype(f32)
        out_ref[:, n * part : (n + 1) * part] = final.astype(out_ref.dtype)

    for n in range(chunks + 4):
        if n < chunks:
            down(n)
        if 0 <= n - 1 < chunks:
            pair(n - 1)
        if 0 <= n - 2 < chunks:
            turn(n - 2)
        if 0 <= n - 3 < chunks:
            across(n - 3)
        if n == chunks:
            counted = jnp.sum(jnp.where(lane == z + 4, route, 0.0), axis=1, keepdims=True)
            row = lax.broadcasted_iota(jnp.int32, (total, LANES), 0)
            per_step = jnp.where(lane == row % steps, counted, 0.0)
            per_step = jnp.sum(per_step, axis=0, keepdims=True).astype(jnp.int32)
            count_ref[...] = per_step[:, :steps]
        if 0 <= n - 4 < chunks:
            finish(n - 4)
    for copy in started:
        copy.wait_send()


def local_gathered(tokens, route_weight, expert_ids, replica, placement, w_gate, w_up, w_down):
    steps, own, width = tokens.shape
    hid = w_gate.shape[2]
    top = expert_ids.shape[2]
    chunks = 4
    part = width // chunks
    block = 4 * steps
    bf16, f32, i32 = jnp.bfloat16, jnp.float32, jnp.int32
    vmem = pl.BlockSpec(memory_space=pltpu.VMEM)
    anywhere = pl.BlockSpec(memory_space=pl.ANY)
    out, count = pl.pallas_call(
        functools.partial(moe_kernel, chunks),
        out_shape=(
            jax.ShapeDtypeStruct((steps, width), bf16),
            jax.ShapeDtypeStruct((1, steps), i32),
        ),
        in_specs=[anywhere] * 8,
        out_specs=(vmem, vmem),
        scratch_shapes=[
            pltpu.VMEM((top, steps), bf16),
            pltpu.VMEM((top, steps), i32),
            pltpu.VMEM((top, steps), i32),
            pltpu.VMEM((2, placement.shape[0]), i32),
            pltpu.VMEM((width, 2 * hid), bf16),
            pltpu.VMEM((hid, width), bf16),
            pltpu.VMEM((steps, LANES), bf16),
            pltpu.VMEM((chunks, 4, steps, part), bf16),
            pltpu.VMEM((4, steps, LANES), bf16),
            pltpu.VMEM((8, block, width + LANES), bf16),
            pltpu.VMEM((chunks, 4, block, part), f32),
            pltpu.VMEM((chunks, 4, block, part), bf16),
            pltpu.VMEM((chunks, 4, block, part), bf16),
            pltpu.VMEM((chunks, 2, block, part), bf16),
            pltpu.VMEM((chunks, block, part), bf16),
            pltpu.VMEM((chunks, 2, block, part), bf16),
            pltpu.VMEM((chunks, block, part), bf16),
            pltpu.VMEM((chunks, 4, steps, part), bf16),
            pltpu.VMEM((chunks, 3, steps, part), bf16),
            pltpu.SemaphoreType.DMA((7 + chunks,)),
            pltpu.SemaphoreType.DMA((17 * chunks + 3,)),
            pltpu.SemaphoreType.DMA((17 * chunks + 3,)),
        ],
        compiler_params=pltpu.CompilerParams(
            collective_id=0, has_side_effects=True, vmem_limit_bytes=VMEM_LIMIT
        ),
    )(
        tokens.reshape(steps, width),
        route_weight.reshape(steps, top).T,
        expert_ids.reshape(steps, top).T,
        replica.reshape(steps, top).T,
        placement.T,
        w_gate,
        w_up,
        w_down,
    )
    return out.reshape(steps, own, width), count.reshape(steps, 1)


def solution(mesh):
    dense = mesh.shape["ep"] == 8 and mesh.shape["dp"] == 4
    return jax.shard_map(
        local_gathered if dense else local_packed,
        mesh=mesh,
        in_specs=(
            P(None, ("ep", "dp"), None),
            P(None, ("ep", "dp"), None),
            P(None, ("ep", "dp"), None),
            P(None, ("ep", "dp"), None),
            P(),
            P("ep", None, "dp"),
            P("ep", None, "dp"),
            P("ep", "dp", None),
        ),
        out_specs=(P(None, ("ep", "dp"), None), P(None, "ep")),
        check_vma=False,
    )
```

```python
import functools

import jax
import jax.numpy as jnp
from jax import lax
from jax.experimental import pallas as pl
from jax.experimental.pallas import tpu as pltpu
from jax.sharding import PartitionSpec as P

MESH = pl.DeviceIdType.MESH
LANES = 128
VMEM_LIMIT = 60 * 1024 * 1024


def pick_slots(expert_ids, replica, placement):
    logical = placement.shape[0]
    chosen = jnp.where(replica[..., None] == 0, placement[:, 0], placement[:, 1])
    matches = expert_ids[..., None] == jnp.arange(logical, dtype=jnp.int32)
    return jnp.sum(jnp.where(matches, chosen, 0), axis=-1)


def place_rows(group_slots, slot_count):
    flat_slots = group_slots.reshape(-1)
    matches = (flat_slots[:, None] == jnp.arange(slot_count, dtype=jnp.int32)[None, :]).astype(
        jnp.int32
    )
    earlier = jnp.cumsum(matches, axis=0) - matches
    position = jnp.sum(earlier * matches, axis=1)
    counts = jnp.sum(matches, axis=0)
    return (position.reshape(group_slots.shape), counts)


def pack_rows(rows, slots, slot_count, capacity, top_count):
    position, counts = place_rows(slots, slot_count)
    target = (slots * capacity + position).reshape(-1)
    repeated = jnp.repeat(rows, top_count, axis=0)
    packed = jnp.zeros((slot_count * capacity, rows.shape[1]), rows.dtype).at[target].set(repeated)
    return (packed.reshape(slot_count, capacity, rows.shape[1]), target)


def expert_block(expert_rows, w_gate, w_up, w_down):
    gate_out = jnp.dot(expert_rows, w_gate[0], preferred_element_type=jnp.float32)
    up_out = jnp.dot(expert_rows, w_up[0], preferred_element_type=jnp.float32)
    hidden = (jax.nn.silu(gate_out) * up_out).astype(jnp.bfloat16)
    return jnp.dot(hidden, w_down[0], preferred_element_type=jnp.float32).astype(jnp.bfloat16)


def combine_rows(
    returned, target, weight_rows, row_count, top_count, slot_count, capacity, model_width
):
    paired = returned.reshape(slot_count, 2, capacity, model_width)
    first_half = paired[:, 0].reshape(-1, model_width)[target].astype(jnp.float32)
    second_half = paired[:, 1].reshape(-1, model_width)[target].astype(jnp.float32)
    weighted = (first_half + second_half) * weight_rows.reshape(-1, 1).astype(jnp.float32)
    return jnp.sum(weighted.reshape(row_count, top_count, model_width), axis=1)


def local_packed(tokens, route_weight, expert_ids, replica, placement, w_gate, w_up, w_down):
    steps_total = tokens.shape[0]
    model_width = tokens.shape[2]
    ep_count = lax.axis_size("ep")
    dp_count = lax.axis_size("dp")
    slot_count = ep_count // 2
    logical = placement.shape[0]
    top_count = expert_ids.shape[2]
    own_count = expert_ids.shape[1]
    group_size = own_count * dp_count
    capacity = 2 * ((group_size * top_count + logical) // (2 * logical)) + 2
    own_slots = pick_slots(expert_ids, replica, placement)
    outputs = []
    load_rows = []
    for step_index in range(steps_total):
        group_slots = lax.all_gather(own_slots[step_index], "dp", axis=0, tiled=True)
        group_counts = place_rows(group_slots, slot_count)[1]
        arrived_counts = lax.all_to_all(
            jnp.repeat(group_counts, 2), "ep", split_axis=0, concat_axis=0, tiled=True
        )
        grouped, group_weight = (
            lax.all_gather(tokens[step_index], "dp", axis=0, tiled=True),
            lax.all_gather(route_weight[step_index], "dp", axis=0, tiled=True),
        )
        send_rows, target = pack_rows(grouped, group_slots, slot_count, capacity, top_count)
        arrived = lax.all_to_all(
            jnp.repeat(send_rows, 2, axis=0), "ep", split_axis=0, concat_axis=0, tiled=True
        )
        block_out = expert_block(arrived.reshape(-1, model_width), w_gate, w_up, w_down)
        returned = lax.all_to_all(
            block_out.reshape(ep_count, capacity, model_width),
            "ep",
            split_axis=0,
            concat_axis=0,
            tiled=True,
        )
        partial_tokens = combine_rows(
            returned, target, group_weight, group_size, top_count, slot_count, capacity, model_width
        )
        token_out = lax.psum_scatter(partial_tokens, "dp", scatter_dimension=0, tiled=True)
        outputs.append(token_out.astype(jnp.bfloat16))
        load_rows.append(jnp.sum(arrived_counts).reshape(1))
    return (jnp.stack(outputs), jnp.stack(load_rows))


def moe_kernel(
    chunks,
    tok_ref,
    rw_ref,
    ids_ref,
    rep_ref,
    place_ref,
    w_gate_ref,
    w_up_ref,
    w_down_ref,
    out_ref,
    count_ref,
    rw,
    ids,
    rep,
    place,
    wgu,
    wd,
    extra,
    zbuf,
    zextra,
    gx,
    ps,
    cs,
    cr,
    first_s,
    second_s,
    first_r,
    second_r,
    tbuf,
    zr,
    wsem,
    ssem,
    rsem,
):
    ep, dp = lax.axis_index("ep"), lax.axis_index("dp")
    z, y = ep // 2, ep % 2
    x, c = dp // 2, dp % 2
    steps, width = tok_ref.shape
    hid = w_gate_ref.shape[2]
    part = width // chunks
    block = 4 * steps
    total = 8 * block
    f32, bf16 = jnp.float32, jnp.bfloat16

    def columns(n, more=0):
        return pl.ds(n * part, part + more)

    def load(src, dst, n):
        copy = pltpu.make_async_copy(src, dst, wsem.at[n])
        copy.start()
        return copy

    small = [
        load(src, dst, n)
        for n, (src, dst) in enumerate(
            [(rw_ref, rw), (ids_ref, ids), (rep_ref, rep), (place_ref, place)]
        )
    ]
    own = [load(tok_ref.at[:, columns(n)], zbuf.at[n, 0], 4 + n) for n in range(chunks)]
    weights = [
        load(w_gate_ref.at[0], wgu.at[:, pl.ds(0, hid)], 4 + chunks),
        load(w_up_ref.at[0], wgu.at[:, pl.ds(hid, hid)], 5 + chunks),
        load(w_down_ref.at[0], wd, 6 + chunks),
    ]

    def device(zz, yy, xx, cc):
        return (zz * 2 + yy, xx * 2 + cc)

    z_others = [z + 1 - 2 * (z % 2), (z + 2) % 4, 3 - z]
    z_dev = [device(zz, y, x, c) for zz in z_others]
    core_dev = device(z, y, x, 1 - c)
    first_dev = device(z, y + c * (1 - 2 * y), x + (1 - c) * (1 - 2 * x), c)
    second_dev = device(z, y + (1 - c) * (1 - 2 * y), x + c * (1 - 2 * x), c)
    slot_a, slot_b = 2 - c, 1 + c

    barrier = pltpu.get_barrier_semaphore()
    partners = z_dev + [core_dev, first_dev, second_dev]
    for partner in partners:
        pl.semaphore_signal(barrier, inc=1, device_id=partner, device_id_type=MESH)
    pl.semaphore_wait(barrier, len(partners))

    started = []

    def send(src, dst, to):
        n = len(started)
        copy = pltpu.make_async_remote_copy(
            src_ref=src,
            dst_ref=dst,
            send_sem=ssem.at[n],
            recv_sem=rsem.at[n],
            device_id=to,
            device_id_type=MESH,
        )
        copy.start()
        started.append(copy)
        return copy

    z_in = [
        [send(tok_ref.at[:, columns(n)], zbuf.at[n, k + 1], z_dev[k]) for k in (2, 1, 0)]
        for n in range(chunks)
    ]

    for copy in small:
        copy.wait()
    lane = lax.broadcasted_iota(jnp.int32, (steps, LANES), 1)
    diagonal = lax.broadcasted_iota(jnp.int32, (steps, steps), 0) == lax.broadcasted_iota(
        jnp.int32, (steps, steps), 1
    )
    slots = jnp.zeros(ids.shape, jnp.int32)
    for e in range(place.shape[1]):
        chosen = jnp.where(rep[...] == 0, place[0:1, e : e + 1], place[1:2, e : e + 1])
        slots = slots + jnp.where(ids[...] == e, chosen, 0)
    packed = jnp.zeros((steps, LANES), f32)
    for k in range(ids.shape[0]):
        slot = jnp.sum(jnp.where(diagonal, slots[k : k + 1], 0), axis=1, keepdims=True)
        gain = rw[k : k + 1].astype(f32)
        gain = jnp.sum(jnp.where(diagonal, gain, 0.0), axis=1, keepdims=True)
        packed = packed + jnp.where(lane == slot, gain, 0.0)
        packed = packed + jnp.where(lane == slot + 4, 1.0, 0.0)
    extra[...] = packed.astype(bf16)
    z_in.append([send(extra, zextra.at[k + 1], z_dev[k]) for k in (2, 1, 0)])

    def span(n):
        return columns(n, LANES if n == chunks - 1 else 0)

    first_in, second_in, core_in, diag_in = {}, {}, {}, {}

    def spread(n):
        own[n].wait()
        for copy in z_in[n]:
            copy.wait_recv()
        gx[0, :, n * part : (n + 1) * part] = jnp.concatenate(
            [zbuf[n, k] for k in range(4)], axis=0
        )
        if n == chunks - 1:
            for copy in z_in[chunks]:
                copy.wait_recv()
            gx[0, :, width : width + LANES] = jnp.concatenate(
                [extra[...]] + [zextra[k] for k in range(1, 4)], axis=0
            )
        here = gx.at[0, :, span(n)]
        first_in[n] = send(here, gx.at[slot_a, :, span(n)], first_dev)
        second_in[n] = send(here, gx.at[slot_b, :, span(n)], second_dev)
        core_in[n] = [send(here, gx.at[4, :, span(n)], core_dev)]

    def forward(n):
        first_in[n].wait_recv()
        here = gx.at[slot_a, :, span(n)]
        diag_in[n] = send(here, gx.at[3, :, span(n)], second_dev)
        core_in[n].append(send(here, gx.at[4 + slot_a, :, span(n)], core_dev))
        second_in[n].wait_recv()
        here = gx.at[slot_b, :, span(n)]
        core_in[n].append(send(here, gx.at[4 + slot_b, :, span(n)], core_dev))

    def corner(n):
        diag_in[n].wait_recv()
        core_in[n].append(send(gx.at[3, :, span(n)], gx.at[7, :, span(n)], core_dev))

    def multiply(n, both):
        if n == 0:
            weights[0].wait()
            weights[1].wait()
        for copy in core_in[n]:
            copy.wait_recv()
        rows = gx[:, :, n * part : (n + 1) * part].reshape(total, part)
        more = jnp.dot(rows, wgu[n * part : (n + 1) * part], preferred_element_type=f32)
        return more if both is None else both + more

    both = None
    for n in range(chunks + 3):
        if n < chunks:
            spread(n)
        if 0 <= n - 1 < chunks:
            forward(n - 1)
        if 0 <= n - 2 < chunks:
            corner(n - 2)
        if 0 <= n - 3 < chunks:
            both = multiply(n - 3, both)

    gate, up = both[:, :hid], both[:, hid:]
    hidden = (gate / (1.0 + jnp.exp(-gate)) * up).astype(bf16)
    route = gx[:, :, width : width + LANES].reshape(total, LANES).astype(f32)
    lane = lax.broadcasted_iota(jnp.int32, (total, LANES), 1)
    weight = jnp.sum(jnp.where(lane == z, route, 0.0), axis=1, keepdims=True)
    weights[2].wait()

    half = total // 2
    to_core, diag_out, first_out, second_out, z_out = {}, {}, {}, {}, {}

    def down(n):
        made = jnp.dot(hidden, wd[:, n * part : (n + 1) * part], preferred_element_type=f32)
        made = made * weight
        cs[n] = made[half:].astype(bf16).reshape(4, block, part)
        to_core[n] = send(cs.at[n], cr.at[n], core_dev)
        ps[n] = made[:half].reshape(4, block, part)

    def pair(n):
        to_core[n].wait_recv()
        first_s[n, 0] = (ps[n, 3] + cr[n, 3].astype(f32)).astype(bf16)
        diag_out[n] = send(first_s.at[n, 0], first_r.at[n, 0], first_dev)
        first_s[n, 1] = (ps[n, slot_a] + cr[n, slot_a].astype(f32)).astype(bf16)
        first_out[n] = send(first_s.at[n, 1], first_r.at[n, 1], first_dev)

    def turn(n):
        held = ps[n, slot_b] + cr[n, slot_b].astype(f32)
        diag_out[n].wait_recv()
        second_s[n] = (held + first_r[n, 0].astype(f32)).astype(bf16)
        second_out[n] = send(second_s.at[n], second_r.at[n], second_dev)

    def across(n):
        held = ps[n, 0] + cr[n, 0].astype(f32)
        first_out[n].wait_recv()
        held = held + first_r[n, 1].astype(f32)
        second_out[n].wait_recv()
        held = (held + second_r[n].astype(f32)).astype(bf16)
        for k in range(4):
            tbuf[n, k] = held[k * steps : (k + 1) * steps]
        z_out[n] = [send(tbuf.at[n, k + 1], zr.at[n, k], z_dev[k]) for k in (2, 1, 0)]

    def finish(n):
        final = tbuf[n, 0].astype(f32)
        for copy in z_out[n]:
            copy.wait_recv()
        for k in range(3):
            final = final + zr[n, k].astype(f32)
        out_ref[:, n * part : (n + 1) * part] = final.astype(out_ref.dtype)

    for n in range(chunks + 4):
        if n < chunks:
            down(n)
        if 0 <= n - 1 < chunks:
            pair(n - 1)
        if 0 <= n - 2 < chunks:
            turn(n - 2)
        if 0 <= n - 3 < chunks:
            across(n - 3)
        if n == chunks:
            counted = jnp.sum(jnp.where(lane == z + 4, route, 0.0), axis=1, keepdims=True)
            row = lax.broadcasted_iota(jnp.int32, (total, LANES), 0)
            per_step = jnp.where(lane == row % steps, counted, 0.0)
            per_step = jnp.sum(per_step, axis=0, keepdims=True).astype(jnp.int32)
            count_ref[...] = per_step[:, :steps]
        if 0 <= n - 4 < chunks:
            finish(n - 4)
    for copy in started:
        copy.wait_send()


def local_gathered(tokens, route_weight, expert_ids, replica, placement, w_gate, w_up, w_down):
    steps, own, width = tokens.shape
    hid = w_gate.shape[2]
    top = expert_ids.shape[2]
    chunks = 1
    part = width // chunks
    block = 4 * steps
    bf16, f32, i32 = jnp.bfloat16, jnp.float32, jnp.int32
    vmem = pl.BlockSpec(memory_space=pltpu.VMEM)
    anywhere = pl.BlockSpec(memory_space=pl.ANY)
    out, count = pl.pallas_call(
        functools.partial(moe_kernel, chunks),
        out_shape=(
            jax.ShapeDtypeStruct((steps, width), bf16),
            jax.ShapeDtypeStruct((1, steps), i32),
        ),
        in_specs=[anywhere] * 8,
        out_specs=(vmem, vmem),
        scratch_shapes=[
            pltpu.VMEM((top, steps), bf16),
            pltpu.VMEM((top, steps), i32),
            pltpu.VMEM((top, steps), i32),
            pltpu.VMEM((2, placement.shape[0]), i32),
            pltpu.VMEM((width, 2 * hid), bf16),
            pltpu.VMEM((hid, width), bf16),
            pltpu.VMEM((steps, LANES), bf16),
            pltpu.VMEM((chunks, 4, steps, part), bf16),
            pltpu.VMEM((4, steps, LANES), bf16),
            pltpu.VMEM((8, block, width + LANES), bf16),
            pltpu.VMEM((chunks, 4, block, part), f32),
            pltpu.VMEM((chunks, 4, block, part), bf16),
            pltpu.VMEM((chunks, 4, block, part), bf16),
            pltpu.VMEM((chunks, 2, block, part), bf16),
            pltpu.VMEM((chunks, block, part), bf16),
            pltpu.VMEM((chunks, 2, block, part), bf16),
            pltpu.VMEM((chunks, block, part), bf16),
            pltpu.VMEM((chunks, 4, steps, part), bf16),
            pltpu.VMEM((chunks, 3, steps, part), bf16),
            pltpu.SemaphoreType.DMA((7 + chunks,)),
            pltpu.SemaphoreType.DMA((17 * chunks + 3,)),
            pltpu.SemaphoreType.DMA((17 * chunks + 3,)),
        ],
        compiler_params=pltpu.CompilerParams(
            collective_id=0, has_side_effects=True, vmem_limit_bytes=VMEM_LIMIT
        ),
    )(
        tokens.reshape(steps, width),
        route_weight.reshape(steps, top).T,
        expert_ids.reshape(steps, top).T,
        replica.reshape(steps, top).T,
        placement.T,
        w_gate,
        w_up,
        w_down,
    )
    return out.reshape(steps, own, width), count.reshape(steps, 1)


def solution(mesh):
    dense = mesh.shape["ep"] == 8 and mesh.shape["dp"] == 4
    return jax.shard_map(
        local_gathered if dense else local_packed,
        mesh=mesh,
        in_specs=(
            P(None, ("ep", "dp"), None),
            P(None, ("ep", "dp"), None),
            P(None, ("ep", "dp"), None),
            P(None, ("ep", "dp"), None),
            P(),
            P("ep", None, "dp"),
            P("ep", None, "dp"),
            P("ep", "dp", None),
        ),
        out_specs=(P(None, ("ep", "dp"), None), P(None, "ep")),
        check_vma=False,
    )
```

```python
import functools

import jax
import jax.numpy as jnp
from jax import lax
from jax.experimental import pallas as pl
from jax.experimental.pallas import tpu as pltpu
from jax.sharding import PartitionSpec as P

MESH = pl.DeviceIdType.MESH
LANES = 128
VMEM_LIMIT = 60 * 1024 * 1024


def pick_slots(expert_ids, replica, placement):
    logical = placement.shape[0]
    chosen = jnp.where(replica[..., None] == 0, placement[:, 0], placement[:, 1])
    matches = expert_ids[..., None] == jnp.arange(logical, dtype=jnp.int32)
    return jnp.sum(jnp.where(matches, chosen, 0), axis=-1)


def place_rows(group_slots, slot_count):
    flat_slots = group_slots.reshape(-1)
    matches = (flat_slots[:, None] == jnp.arange(slot_count, dtype=jnp.int32)[None, :]).astype(
        jnp.int32
    )
    earlier = jnp.cumsum(matches, axis=0) - matches
    position = jnp.sum(earlier * matches, axis=1)
    counts = jnp.sum(matches, axis=0)
    return (position.reshape(group_slots.shape), counts)


def pack_rows(rows, slots, slot_count, capacity, top_count):
    position, counts = place_rows(slots, slot_count)
    target = (slots * capacity + position).reshape(-1)
    repeated = jnp.repeat(rows, top_count, axis=0)
    packed = jnp.zeros((slot_count * capacity, rows.shape[1]), rows.dtype).at[target].set(repeated)
    return (packed.reshape(slot_count, capacity, rows.shape[1]), target)


def expert_block(expert_rows, w_gate, w_up, w_down):
    gate_out = jnp.dot(expert_rows, w_gate[0], preferred_element_type=jnp.float32)
    up_out = jnp.dot(expert_rows, w_up[0], preferred_element_type=jnp.float32)
    hidden = (jax.nn.silu(gate_out) * up_out).astype(jnp.bfloat16)
    return jnp.dot(hidden, w_down[0], preferred_element_type=jnp.float32).astype(jnp.bfloat16)


def combine_rows(
    returned, target, weight_rows, row_count, top_count, slot_count, capacity, model_width
):
    paired = returned.reshape(slot_count, 2, capacity, model_width)
    first_half = paired[:, 0].reshape(-1, model_width)[target].astype(jnp.float32)
    second_half = paired[:, 1].reshape(-1, model_width)[target].astype(jnp.float32)
    weighted = (first_half + second_half) * weight_rows.reshape(-1, 1).astype(jnp.float32)
    return jnp.sum(weighted.reshape(row_count, top_count, model_width), axis=1)


def local_packed(tokens, route_weight, expert_ids, replica, placement, w_gate, w_up, w_down):
    steps_total = tokens.shape[0]
    model_width = tokens.shape[2]
    ep_count = lax.axis_size("ep")
    dp_count = lax.axis_size("dp")
    slot_count = ep_count // 2
    logical = placement.shape[0]
    top_count = expert_ids.shape[2]
    own_count = expert_ids.shape[1]
    group_size = own_count * dp_count
    capacity = 2 * ((group_size * top_count + logical) // (2 * logical)) + 2
    own_slots = pick_slots(expert_ids, replica, placement)
    outputs = []
    load_rows = []
    for step_index in range(steps_total):
        group_slots = lax.all_gather(own_slots[step_index], "dp", axis=0, tiled=True)
        group_counts = place_rows(group_slots, slot_count)[1]
        arrived_counts = lax.all_to_all(
            jnp.repeat(group_counts, 2), "ep", split_axis=0, concat_axis=0, tiled=True
        )
        grouped, group_weight = (
            lax.all_gather(tokens[step_index], "dp", axis=0, tiled=True),
            lax.all_gather(route_weight[step_index], "dp", axis=0, tiled=True),
        )
        send_rows, target = pack_rows(grouped, group_slots, slot_count, capacity, top_count)
        arrived = lax.all_to_all(
            jnp.repeat(send_rows, 2, axis=0), "ep", split_axis=0, concat_axis=0, tiled=True
        )
        block_out = expert_block(arrived.reshape(-1, model_width), w_gate, w_up, w_down)
        returned = lax.all_to_all(
            block_out.reshape(ep_count, capacity, model_width),
            "ep",
            split_axis=0,
            concat_axis=0,
            tiled=True,
        )
        partial_tokens = combine_rows(
            returned, target, group_weight, group_size, top_count, slot_count, capacity, model_width
        )
        token_out = lax.psum_scatter(partial_tokens, "dp", scatter_dimension=0, tiled=True)
        outputs.append(token_out.astype(jnp.bfloat16))
        load_rows.append(jnp.sum(arrived_counts).reshape(1))
    return (jnp.stack(outputs), jnp.stack(load_rows))


def moe_kernel(
    chunks,
    tok_ref,
    rw_ref,
    ids_ref,
    rep_ref,
    place_ref,
    w_gate_ref,
    w_up_ref,
    w_down_ref,
    out_ref,
    count_ref,
    rw,
    ids,
    rep,
    place,
    wgu,
    wd,
    zbuf,
    gx,
    ps,
    cs,
    cr,
    qs,
    qr,
    tbuf,
    zr,
    wsem,
    ssem,
    rsem,
):
    ep, dp = lax.axis_index("ep"), lax.axis_index("dp")
    z, y = ep // 2, ep % 2
    x, c = dp // 2, dp % 2
    steps, width = tok_ref.shape
    hid = w_gate_ref.shape[2]
    part = width // chunks
    block = 4 * steps
    total = 8 * block
    f32, bf16 = jnp.float32, jnp.bfloat16

    def columns(n, more=0):
        return pl.ds(n * part, part + more)

    def load(src, dst, n):
        copy = pltpu.make_async_copy(src, dst, wsem.at[n])
        copy.start()
        return copy

    small = [
        load(src, dst, n)
        for n, (src, dst) in enumerate(
            [(rw_ref, rw), (ids_ref, ids), (rep_ref, rep), (place_ref, place)]
        )
    ]
    own = [
        load(tok_ref.at[:, columns(n)], zbuf.at[n, 0, :, pl.ds(0, part)], 4 + n)
        for n in range(chunks)
    ]
    weights = [
        load(w_gate_ref.at[0], wgu.at[:, pl.ds(0, hid)], 4 + chunks),
        load(w_up_ref.at[0], wgu.at[:, pl.ds(hid, hid)], 5 + chunks),
        load(w_down_ref.at[0], wd, 6 + chunks),
    ]

    def device(zz, yy, xx, cc):
        return (zz * 2 + yy, xx * 2 + cc)

    z_others = [z + 1 - 2 * (z % 2), (z + 2) % 4, 3 - z]
    z_dev = [device(zz, y, x, c) for zz in z_others]
    core_dev = device(z, y, x, 1 - c)
    x_dev = device(z, y, 1 - x, c)
    y_dev = device(z, 1 - y, x, c)
    far_dev = device(z, 1 - y, 1 - x, c)
    plane = [(3, far_dev), (2, x_dev), (1, y_dev)]

    barrier = pltpu.get_barrier_semaphore()
    partners = z_dev + [core_dev, x_dev, y_dev, far_dev]
    for partner in partners:
        pl.semaphore_signal(barrier, inc=1, device_id=partner, device_id_type=MESH)

    started = []

    def send(src, dst, to):
        n = len(started)
        copy = pltpu.make_async_remote_copy(
            src_ref=src,
            dst_ref=dst,
            send_sem=ssem.at[n],
            recv_sem=rsem.at[n],
            device_id=to,
            device_id_type=MESH,
        )
        copy.start()
        started.append(copy)
        return copy

    for copy in small:
        copy.wait()
    lane = lax.broadcasted_iota(jnp.int32, (steps, LANES), 1)
    diagonal = lax.broadcasted_iota(jnp.int32, (steps, steps), 0) == lax.broadcasted_iota(
        jnp.int32, (steps, steps), 1
    )
    slots = jnp.zeros(ids.shape, jnp.int32)
    for e in range(place.shape[1]):
        chosen = jnp.where(rep[...] == 0, place[0:1, e : e + 1], place[1:2, e : e + 1])
        slots = slots + jnp.where(ids[...] == e, chosen, 0)
    packed = jnp.zeros((steps, LANES), f32)
    for k in range(ids.shape[0]):
        slot = jnp.sum(jnp.where(diagonal, slots[k : k + 1], 0), axis=1, keepdims=True)
        gain = rw[k : k + 1].astype(f32)
        gain = jnp.sum(jnp.where(diagonal, gain, 0.0), axis=1, keepdims=True)
        packed = packed + jnp.where(lane == slot, gain, 0.0)
        packed = packed + jnp.where(lane == slot + 4, 1.0, 0.0)
    zbuf[chunks - 1, 0, :, part:] = packed.astype(bf16)
    for copy in own:
        copy.wait()
    pl.semaphore_wait(barrier, len(partners))

    def wide(n):
        return pl.ds(0, part + (LANES if n == chunks - 1 else 0))

    def span(n):
        return columns(n, LANES if n == chunks - 1 else 0)

    z_in = [
        [
            send(zbuf.at[n, 0, :, wide(n)], zbuf.at[n, k + 1, :, wide(n)], z_dev[k])
            for k in (2, 1, 0)
        ]
        for n in range(chunks)
    ]

    plane_in, core_in = {}, {}

    def spread(n):
        for copy in z_in[n]:
            copy.wait_recv()
        end = part + (LANES if n == chunks - 1 else 0)
        gx[0, :, n * part : n * part + end] = jnp.concatenate(
            [zbuf[n, k, :, 0:end] for k in range(4)], axis=0
        )
        here = gx.at[0, :, span(n)]
        plane_in[n] = [send(here, gx.at[i, :, span(n)], to) for i, to in plane]
        core_in[n] = [send(here, gx.at[4, :, span(n)], core_dev)]

    def forward(n):
        for copy in plane_in[n]:
            copy.wait_recv()
        core_in[n].append(
            send(gx.at[pl.ds(1, 3), :, span(n)], gx.at[pl.ds(5, 3), :, span(n)], core_dev)
        )

    def multiply(n, both):
        if n == 0:
            weights[0].wait()
            weights[1].wait()
        for copy in core_in[n]:
            copy.wait_recv()
        rows = gx[:, :, n * part : (n + 1) * part].reshape(total, part)
        more = jnp.dot(rows, wgu[n * part : (n + 1) * part], preferred_element_type=f32)
        return more if both is None else both + more

    both = None
    for n in range(chunks + 2):
        if n < chunks:
            spread(n)
        if 0 <= n - 1 < chunks:
            forward(n - 1)
        if 0 <= n - 2 < chunks:
            both = multiply(n - 2, both)

    gate, up = both[:, :hid], both[:, hid:]
    hidden = (gate / (1.0 + jnp.exp(-gate)) * up).astype(bf16)
    route = gx[:, :, width : width + LANES].reshape(total, LANES).astype(f32)
    lane = lax.broadcasted_iota(jnp.int32, (total, LANES), 1)
    weight = jnp.sum(jnp.where(lane == z, route, 0.0), axis=1, keepdims=True)
    weights[2].wait()

    half = total // 2
    to_core, plane_out, z_out = {}, {}, {}

    def down(n):
        held = wd[:, n * part : (n + 1) * part]
        theirs = jnp.dot(hidden[half:], held, preferred_element_type=f32) * weight[half:]
        cs[n] = theirs.astype(bf16).reshape(4, block, part)
        to_core[n] = send(cs.at[n], cr.at[n], core_dev)
        mine = jnp.dot(hidden[:half], held, preferred_element_type=f32) * weight[:half]
        ps[n] = mine.reshape(4, block, part)

    def pair(n):
        to_core[n].wait_recv()
        plane_out[n] = []
        for i, to in plane:
            qs[n, i - 1] = (ps[n, i] + cr[n, i].astype(f32)).astype(bf16)
            plane_out[n].append(send(qs.at[n, i - 1], qr.at[n, i - 1], to))

    def across(n):
        held = ps[n, 0] + cr[n, 0].astype(f32)
        for (i, _), copy in zip(reversed(plane), reversed(plane_out[n])):
            copy.wait_recv()
            held = held + qr[n, i - 1].astype(f32)
        held = held.astype(bf16)
        for k in range(4):
            tbuf[n, k] = held[k * steps : (k + 1) * steps]
        z_out[n] = [send(tbuf.at[n, k + 1], zr.at[n, k], z_dev[k]) for k in (2, 1, 0)]

    def finish(n):
        final = tbuf[n, 0].astype(f32)
        for copy in z_out[n]:
            copy.wait_recv()
        for k in range(3):
            final = final + zr[n, k].astype(f32)
        out_ref[:, n * part : (n + 1) * part] = final.astype(out_ref.dtype)

    for n in range(chunks + 3):
        if n < chunks:
            down(n)
        if 0 <= n - 1 < chunks:
            pair(n - 1)
        if 0 <= n - 2 < chunks:
            across(n - 2)
        if n == chunks:
            counted = jnp.sum(jnp.where(lane == z + 4, route, 0.0), axis=1, keepdims=True)
            row = lax.broadcasted_iota(jnp.int32, (total, LANES), 0)
            per_step = jnp.where(lane == row % steps, counted, 0.0)
            per_step = jnp.sum(per_step, axis=0, keepdims=True).astype(jnp.int32)
            count_ref[...] = per_step[:, :steps]
        if 0 <= n - 3 < chunks:
            finish(n - 3)
    for copy in started:
        copy.wait_send()


def local_gathered(tokens, route_weight, expert_ids, replica, placement, w_gate, w_up, w_down):
    steps, own, width = tokens.shape
    hid = w_gate.shape[2]
    top = expert_ids.shape[2]
    chunks = 1
    part = width // chunks
    block = 4 * steps
    bf16, f32, i32 = jnp.bfloat16, jnp.float32, jnp.int32
    vmem = pl.BlockSpec(memory_space=pltpu.VMEM)
    anywhere = pl.BlockSpec(memory_space=pl.ANY)
    out, count = pl.pallas_call(
        functools.partial(moe_kernel, chunks),
        out_shape=(
            jax.ShapeDtypeStruct((steps, width), bf16),
            jax.ShapeDtypeStruct((1, steps), i32),
        ),
        in_specs=[anywhere] * 8,
        out_specs=(vmem, vmem),
        scratch_shapes=[
            pltpu.VMEM((top, steps), bf16),
            pltpu.VMEM((top, steps), i32),
            pltpu.VMEM((top, steps), i32),
            pltpu.VMEM((2, placement.shape[0]), i32),
            pltpu.VMEM((width, 2 * hid), bf16),
            pltpu.VMEM((hid, width), bf16),
            pltpu.VMEM((chunks, 4, steps, part + LANES), bf16),
            pltpu.VMEM((8, block, width + LANES), bf16),
            pltpu.VMEM((chunks, 4, block, part), f32),
            pltpu.VMEM((chunks, 4, block, part), bf16),
            pltpu.VMEM((chunks, 4, block, part), bf16),
            pltpu.VMEM((chunks, 3, block, part), bf16),
            pltpu.VMEM((chunks, 3, block, part), bf16),
            pltpu.VMEM((chunks, 4, steps, part), bf16),
            pltpu.VMEM((chunks, 3, steps, part), bf16),
            pltpu.SemaphoreType.DMA((7 + chunks,)),
            pltpu.SemaphoreType.DMA((15 * chunks,)),
            pltpu.SemaphoreType.DMA((15 * chunks,)),
        ],
        compiler_params=pltpu.CompilerParams(
            collective_id=0, has_side_effects=True, vmem_limit_bytes=VMEM_LIMIT
        ),
    )(
        tokens.reshape(steps, width),
        route_weight.reshape(steps, top).T,
        expert_ids.reshape(steps, top).T,
        replica.reshape(steps, top).T,
        placement.T,
        w_gate,
        w_up,
        w_down,
    )
    return out.reshape(steps, own, width), count.reshape(steps, 1)


def solution(mesh):
    dense = mesh.shape["ep"] == 8 and mesh.shape["dp"] == 4
    return jax.shard_map(
        local_gathered if dense else local_packed,
        mesh=mesh,
        in_specs=(
            P(None, ("ep", "dp"), None),
            P(None, ("ep", "dp"), None),
            P(None, ("ep", "dp"), None),
            P(None, ("ep", "dp"), None),
            P(),
            P("ep", None, "dp"),
            P("ep", None, "dp"),
            P("ep", "dp", None),
        ),
        out_specs=(P(None, ("ep", "dp"), None), P(None, "ep")),
        check_vma=False,
    )
```

```python
import functools

import jax
import jax.numpy as jnp
from jax import lax
from jax.experimental import pallas as pl
from jax.experimental.pallas import tpu as pltpu
from jax.sharding import PartitionSpec as P

MESH = pl.DeviceIdType.MESH
LANES = 128
VMEM_LIMIT = 60 * 1024 * 1024


def pick_slots(expert_ids, replica, placement):
    logical = placement.shape[0]
    chosen = jnp.where(replica[..., None] == 0, placement[:, 0], placement[:, 1])
    matches = expert_ids[..., None] == jnp.arange(logical, dtype=jnp.int32)
    return jnp.sum(jnp.where(matches, chosen, 0), axis=-1)


def place_rows(group_slots, slot_count):
    flat_slots = group_slots.reshape(-1)
    matches = (flat_slots[:, None] == jnp.arange(slot_count, dtype=jnp.int32)[None, :]).astype(
        jnp.int32
    )
    earlier = jnp.cumsum(matches, axis=0) - matches
    position = jnp.sum(earlier * matches, axis=1)
    counts = jnp.sum(matches, axis=0)
    return (position.reshape(group_slots.shape), counts)


def pack_rows(rows, slots, slot_count, capacity, top_count):
    position, counts = place_rows(slots, slot_count)
    target = (slots * capacity + position).reshape(-1)
    repeated = jnp.repeat(rows, top_count, axis=0)
    packed = jnp.zeros((slot_count * capacity, rows.shape[1]), rows.dtype).at[target].set(repeated)
    return (packed.reshape(slot_count, capacity, rows.shape[1]), target)


def expert_block(expert_rows, w_gate, w_up, w_down):
    gate_out = jnp.dot(expert_rows, w_gate[0], preferred_element_type=jnp.float32)
    up_out = jnp.dot(expert_rows, w_up[0], preferred_element_type=jnp.float32)
    hidden = (jax.nn.silu(gate_out) * up_out).astype(jnp.bfloat16)
    return jnp.dot(hidden, w_down[0], preferred_element_type=jnp.float32).astype(jnp.bfloat16)


def combine_rows(
    returned, target, weight_rows, row_count, top_count, slot_count, capacity, model_width
):
    paired = returned.reshape(slot_count, 2, capacity, model_width)
    first_half = paired[:, 0].reshape(-1, model_width)[target].astype(jnp.float32)
    second_half = paired[:, 1].reshape(-1, model_width)[target].astype(jnp.float32)
    weighted = (first_half + second_half) * weight_rows.reshape(-1, 1).astype(jnp.float32)
    return jnp.sum(weighted.reshape(row_count, top_count, model_width), axis=1)


def local_packed(tokens, route_weight, expert_ids, replica, placement, w_gate, w_up, w_down):
    steps_total = tokens.shape[0]
    model_width = tokens.shape[2]
    ep_count = lax.axis_size("ep")
    dp_count = lax.axis_size("dp")
    slot_count = ep_count // 2
    logical = placement.shape[0]
    top_count = expert_ids.shape[2]
    own_count = expert_ids.shape[1]
    group_size = own_count * dp_count
    capacity = 2 * ((group_size * top_count + logical) // (2 * logical)) + 2
    own_slots = pick_slots(expert_ids, replica, placement)
    outputs = []
    load_rows = []
    for step_index in range(steps_total):
        group_slots = lax.all_gather(own_slots[step_index], "dp", axis=0, tiled=True)
        group_counts = place_rows(group_slots, slot_count)[1]
        arrived_counts = lax.all_to_all(
            jnp.repeat(group_counts, 2), "ep", split_axis=0, concat_axis=0, tiled=True
        )
        grouped, group_weight = (
            lax.all_gather(tokens[step_index], "dp", axis=0, tiled=True),
            lax.all_gather(route_weight[step_index], "dp", axis=0, tiled=True),
        )
        send_rows, target = pack_rows(grouped, group_slots, slot_count, capacity, top_count)
        arrived = lax.all_to_all(
            jnp.repeat(send_rows, 2, axis=0), "ep", split_axis=0, concat_axis=0, tiled=True
        )
        block_out = expert_block(arrived.reshape(-1, model_width), w_gate, w_up, w_down)
        returned = lax.all_to_all(
            block_out.reshape(ep_count, capacity, model_width),
            "ep",
            split_axis=0,
            concat_axis=0,
            tiled=True,
        )
        partial_tokens = combine_rows(
            returned, target, group_weight, group_size, top_count, slot_count, capacity, model_width
        )
        token_out = lax.psum_scatter(partial_tokens, "dp", scatter_dimension=0, tiled=True)
        outputs.append(token_out.astype(jnp.bfloat16))
        load_rows.append(jnp.sum(arrived_counts).reshape(1))
    return (jnp.stack(outputs), jnp.stack(load_rows))


def moe_kernel(
    chunks,
    tok_ref,
    rw_ref,
    ids_ref,
    rep_ref,
    place_ref,
    w_gate_ref,
    w_up_ref,
    w_down_ref,
    out_ref,
    count_ref,
    rw,
    ids,
    rep,
    place,
    wgu,
    wd,
    zbuf,
    gx,
    ps,
    cs,
    cr,
    qs,
    qr,
    tbuf,
    zr,
    wsem,
    ssem,
    rsem,
):
    ep, dp = lax.axis_index("ep"), lax.axis_index("dp")
    z, y = ep // 2, ep % 2
    x, c = dp // 2, dp % 2
    steps, width = tok_ref.shape
    hid = w_gate_ref.shape[2]
    part = width // chunks
    block = 4 * steps
    total = 8 * block
    f32, bf16 = jnp.float32, jnp.bfloat16

    def columns(n, more=0):
        return pl.ds(n * part, part + more)

    def load(src, dst, n):
        copy = pltpu.make_async_copy(src, dst, wsem.at[n])
        copy.start()
        return copy

    small = [
        load(src, dst, n)
        for n, (src, dst) in enumerate(
            [(rw_ref, rw), (ids_ref, ids), (rep_ref, rep), (place_ref, place)]
        )
    ]
    own = [
        load(tok_ref.at[:, columns(n)], zbuf.at[n, 0, :, pl.ds(0, part)], 4 + n)
        for n in range(chunks)
    ]
    weights = [
        load(w_gate_ref.at[0], wgu.at[:, pl.ds(0, hid)], 4 + chunks),
        load(w_up_ref.at[0], wgu.at[:, pl.ds(hid, hid)], 5 + chunks),
        load(w_down_ref.at[0], wd, 6 + chunks),
    ]

    def device(zz, yy, xx, cc):
        return (zz * 2 + yy, xx * 2 + cc)

    z_others = [z + 1 - 2 * (z % 2), (z + 2) % 4, 3 - z]
    z_dev = [device(zz, y, x, c) for zz in z_others]
    core_dev = device(z, y, x, 1 - c)
    x_dev = device(z, y, 1 - x, c)
    y_dev = device(z, 1 - y, x, c)
    far_dev = device(z, 1 - y, 1 - x, c)
    plane = [(3, far_dev), (2, x_dev), (1, y_dev)]

    barrier = pltpu.get_barrier_semaphore()
    partners = z_dev + [core_dev, x_dev, y_dev, far_dev]
    for partner in partners:
        pl.semaphore_signal(barrier, inc=1, device_id=partner, device_id_type=MESH)

    started = []

    def send(src, dst, to):
        n = len(started)
        copy = pltpu.make_async_remote_copy(
            src_ref=src,
            dst_ref=dst,
            send_sem=ssem.at[n],
            recv_sem=rsem.at[n],
            device_id=to,
            device_id_type=MESH,
        )
        copy.start()
        started.append(copy)
        return copy

    for copy in small:
        copy.wait()
    lane = lax.broadcasted_iota(jnp.int32, (steps, LANES), 1)
    diagonal = lax.broadcasted_iota(jnp.int32, (steps, steps), 0) == lax.broadcasted_iota(
        jnp.int32, (steps, steps), 1
    )
    slots = jnp.zeros(ids.shape, jnp.int32)
    for e in range(place.shape[1]):
        chosen = jnp.where(rep[...] == 0, place[0:1, e : e + 1], place[1:2, e : e + 1])
        slots = slots + jnp.where(ids[...] == e, chosen, 0)
    packed = jnp.zeros((steps, LANES), f32)
    for k in range(ids.shape[0]):
        slot = jnp.sum(jnp.where(diagonal, slots[k : k + 1], 0), axis=1, keepdims=True)
        gain = rw[k : k + 1].astype(f32)
        gain = jnp.sum(jnp.where(diagonal, gain, 0.0), axis=1, keepdims=True)
        packed = packed + jnp.where(lane == slot, gain, 0.0)
        packed = packed + jnp.where(lane == slot + 4, 1.0, 0.0)
    zbuf[chunks - 1, 0, :, part:] = packed.astype(bf16)
    for copy in own:
        copy.wait()
    pl.semaphore_wait(barrier, len(partners))

    def wide(n):
        return pl.ds(0, part + (LANES if n == chunks - 1 else 0))

    def span(n):
        return columns(n, LANES if n == chunks - 1 else 0)

    z_in = [
        [
            send(zbuf.at[n, 0, :, wide(n)], zbuf.at[n, k + 1, :, wide(n)], z_dev[k])
            for k in (2, 1, 0)
        ]
        for n in range(chunks)
    ]

    plane_in, core_in = {}, {}

    def spread(n):
        for copy in z_in[n]:
            copy.wait_recv()
        end = part + (LANES if n == chunks - 1 else 0)
        gx[0, :, n * part : n * part + end] = jnp.concatenate(
            [zbuf[n, k, :, 0:end] for k in range(4)], axis=0
        )
        here = gx.at[0, :, span(n)]
        plane_in[n] = [send(here, gx.at[i, :, span(n)], to) for i, to in plane]
        core_in[n] = [send(here, gx.at[4, :, span(n)], core_dev)]

    def forward(n):
        for copy in plane_in[n]:
            copy.wait_recv()
        core_in[n].append(
            send(gx.at[pl.ds(1, 3), :, span(n)], gx.at[pl.ds(5, 3), :, span(n)], core_dev)
        )

    def multiply(n, both):
        if n == 0:
            weights[0].wait()
            weights[1].wait()
        for copy in core_in[n]:
            copy.wait_recv()
        rows = gx[:, :, n * part : (n + 1) * part].reshape(total, part)
        more = jnp.dot(rows, wgu[n * part : (n + 1) * part], preferred_element_type=f32)
        return more if both is None else both + more

    both = None
    for n in range(chunks + 2):
        if n < chunks:
            spread(n)
        if 0 <= n - 1 < chunks:
            forward(n - 1)
        if 0 <= n - 2 < chunks:
            both = multiply(n - 2, both)

    gate, up = both[:, :hid], both[:, hid:]
    hidden = (gate / (1.0 + jnp.exp(-gate)) * up).astype(bf16)
    route = gx[:, :, width : width + LANES].reshape(total, LANES).astype(f32)
    lane = lax.broadcasted_iota(jnp.int32, (total, LANES), 1)
    weight = jnp.sum(jnp.where(lane == z, route, 0.0), axis=1, keepdims=True)
    weights[2].wait()

    half = total // 2
    to_core, plane_out, z_out = {}, {}, {}

    def down(n):
        held = wd[:, n * part : (n + 1) * part]
        theirs = jnp.dot(hidden[half:], held, preferred_element_type=f32) * weight[half:]
        cs[n] = theirs.astype(bf16).reshape(4, block, part)
        to_core[n] = send(cs.at[n], cr.at[n], core_dev)
        mine = jnp.dot(hidden[:half], held, preferred_element_type=f32) * weight[:half]
        ps[n] = mine.reshape(4, block, part)

    def pair(n):
        to_core[n].wait_recv()
        plane_out[n] = []
        for i, to in plane:
            qs[n, i - 1] = (ps[n, i] + cr[n, i].astype(f32)).astype(bf16)
            plane_out[n].append(send(qs.at[n, i - 1], qr.at[n, i - 1], to))

    def across(n):
        held = ps[n, 0] + cr[n, 0].astype(f32)
        for (i, _), copy in zip(reversed(plane), reversed(plane_out[n])):
            copy.wait_recv()
            held = held + qr[n, i - 1].astype(f32)
        held = held.astype(bf16)
        for k in range(4):
            tbuf[n, k] = held[k * steps : (k + 1) * steps]
        z_out[n] = [send(tbuf.at[n, k + 1], zr.at[n, k], z_dev[k]) for k in (2, 1, 0)]

    def finish(n):
        final = tbuf[n, 0].astype(f32)
        for copy in z_out[n]:
            copy.wait_recv()
        for k in range(3):
            final = final + zr[n, k].astype(f32)
        out_ref[:, n * part : (n + 1) * part] = final.astype(out_ref.dtype)

    for n in range(chunks + 3):
        if n < chunks:
            down(n)
        if 0 <= n - 1 < chunks:
            pair(n - 1)
        if 0 <= n - 2 < chunks:
            across(n - 2)
        if n == chunks:
            counted = jnp.sum(jnp.where(lane == z + 4, route, 0.0), axis=1, keepdims=True)
            row = lax.broadcasted_iota(jnp.int32, (total, LANES), 0)
            per_step = jnp.where(lane == row % steps, counted, 0.0)
            per_step = jnp.sum(per_step, axis=0, keepdims=True).astype(jnp.int32)
            count_ref[...] = per_step[:, :steps]
        if 0 <= n - 3 < chunks:
            finish(n - 3)
    for copy in started:
        copy.wait_send()


def local_gathered(tokens, route_weight, expert_ids, replica, placement, w_gate, w_up, w_down):
    steps, own, width = tokens.shape
    hid = w_gate.shape[2]
    top = expert_ids.shape[2]
    chunks = 2
    part = width // chunks
    block = 4 * steps
    bf16, f32, i32 = jnp.bfloat16, jnp.float32, jnp.int32
    vmem = pl.BlockSpec(memory_space=pltpu.VMEM)
    anywhere = pl.BlockSpec(memory_space=pl.ANY)
    out, count = pl.pallas_call(
        functools.partial(moe_kernel, chunks),
        out_shape=(
            jax.ShapeDtypeStruct((steps, width), bf16),
            jax.ShapeDtypeStruct((1, steps), i32),
        ),
        in_specs=[anywhere] * 8,
        out_specs=(vmem, vmem),
        scratch_shapes=[
            pltpu.VMEM((top, steps), bf16),
            pltpu.VMEM((top, steps), i32),
            pltpu.VMEM((top, steps), i32),
            pltpu.VMEM((2, placement.shape[0]), i32),
            pltpu.VMEM((width, 2 * hid), bf16),
            pltpu.VMEM((hid, width), bf16),
            pltpu.VMEM((chunks, 4, steps, part + LANES), bf16),
            pltpu.VMEM((8, block, width + LANES), bf16),
            pltpu.VMEM((chunks, 4, block, part), f32),
            pltpu.VMEM((chunks, 4, block, part), bf16),
            pltpu.VMEM((chunks, 4, block, part), bf16),
            pltpu.VMEM((chunks, 3, block, part), bf16),
            pltpu.VMEM((chunks, 3, block, part), bf16),
            pltpu.VMEM((chunks, 4, steps, part), bf16),
            pltpu.VMEM((chunks, 3, steps, part), bf16),
            pltpu.SemaphoreType.DMA((7 + chunks,)),
            pltpu.SemaphoreType.DMA((15 * chunks,)),
            pltpu.SemaphoreType.DMA((15 * chunks,)),
        ],
        compiler_params=pltpu.CompilerParams(
            collective_id=0, has_side_effects=True, vmem_limit_bytes=VMEM_LIMIT
        ),
    )(
        tokens.reshape(steps, width),
        route_weight.reshape(steps, top).T,
        expert_ids.reshape(steps, top).T,
        replica.reshape(steps, top).T,
        placement.T,
        w_gate,
        w_up,
        w_down,
    )
    return out.reshape(steps, own, width), count.reshape(steps, 1)


def solution(mesh):
    dense = mesh.shape["ep"] == 8 and mesh.shape["dp"] == 4
    return jax.shard_map(
        local_gathered if dense else local_packed,
        mesh=mesh,
        in_specs=(
            P(None, ("ep", "dp"), None),
            P(None, ("ep", "dp"), None),
            P(None, ("ep", "dp"), None),
            P(None, ("ep", "dp"), None),
            P(),
            P("ep", None, "dp"),
            P("ep", None, "dp"),
            P("ep", "dp", None),
        ),
        out_specs=(P(None, ("ep", "dp"), None), P(None, "ep")),
        check_vma=False,
    )
```

```python
import functools

import jax
import jax.numpy as jnp
from jax import lax
from jax.experimental import pallas as pl
from jax.experimental.pallas import tpu as pltpu
from jax.sharding import PartitionSpec as P

MESH = pl.DeviceIdType.MESH
LANES = 128
VMEM_LIMIT = 60 * 1024 * 1024


def pick_slots(expert_ids, replica, placement):
    logical = placement.shape[0]
    chosen = jnp.where(replica[..., None] == 0, placement[:, 0], placement[:, 1])
    matches = expert_ids[..., None] == jnp.arange(logical, dtype=jnp.int32)
    return jnp.sum(jnp.where(matches, chosen, 0), axis=-1)


def place_rows(group_slots, slot_count):
    flat_slots = group_slots.reshape(-1)
    matches = (flat_slots[:, None] == jnp.arange(slot_count, dtype=jnp.int32)[None, :]).astype(
        jnp.int32
    )
    earlier = jnp.cumsum(matches, axis=0) - matches
    position = jnp.sum(earlier * matches, axis=1)
    counts = jnp.sum(matches, axis=0)
    return (position.reshape(group_slots.shape), counts)


def pack_rows(rows, slots, slot_count, capacity, top_count):
    position, counts = place_rows(slots, slot_count)
    target = (slots * capacity + position).reshape(-1)
    repeated = jnp.repeat(rows, top_count, axis=0)
    packed = jnp.zeros((slot_count * capacity, rows.shape[1]), rows.dtype).at[target].set(repeated)
    return (packed.reshape(slot_count, capacity, rows.shape[1]), target)


def expert_block(expert_rows, w_gate, w_up, w_down):
    gate_out = jnp.dot(expert_rows, w_gate[0], preferred_element_type=jnp.float32)
    up_out = jnp.dot(expert_rows, w_up[0], preferred_element_type=jnp.float32)
    hidden = (jax.nn.silu(gate_out) * up_out).astype(jnp.bfloat16)
    return jnp.dot(hidden, w_down[0], preferred_element_type=jnp.float32).astype(jnp.bfloat16)


def combine_rows(
    returned, target, weight_rows, row_count, top_count, slot_count, capacity, model_width
):
    paired = returned.reshape(slot_count, 2, capacity, model_width)
    first_half = paired[:, 0].reshape(-1, model_width)[target].astype(jnp.float32)
    second_half = paired[:, 1].reshape(-1, model_width)[target].astype(jnp.float32)
    weighted = (first_half + second_half) * weight_rows.reshape(-1, 1).astype(jnp.float32)
    return jnp.sum(weighted.reshape(row_count, top_count, model_width), axis=1)


def local_packed(tokens, route_weight, expert_ids, replica, placement, w_gate, w_up, w_down):
    steps_total = tokens.shape[0]
    model_width = tokens.shape[2]
    ep_count = lax.axis_size("ep")
    dp_count = lax.axis_size("dp")
    slot_count = ep_count // 2
    logical = placement.shape[0]
    top_count = expert_ids.shape[2]
    own_count = expert_ids.shape[1]
    group_size = own_count * dp_count
    capacity = 2 * ((group_size * top_count + logical) // (2 * logical)) + 2
    own_slots = pick_slots(expert_ids, replica, placement)
    outputs = []
    load_rows = []
    for step_index in range(steps_total):
        group_slots = lax.all_gather(own_slots[step_index], "dp", axis=0, tiled=True)
        group_counts = place_rows(group_slots, slot_count)[1]
        arrived_counts = lax.all_to_all(
            jnp.repeat(group_counts, 2), "ep", split_axis=0, concat_axis=0, tiled=True
        )
        grouped, group_weight = (
            lax.all_gather(tokens[step_index], "dp", axis=0, tiled=True),
            lax.all_gather(route_weight[step_index], "dp", axis=0, tiled=True),
        )
        send_rows, target = pack_rows(grouped, group_slots, slot_count, capacity, top_count)
        arrived = lax.all_to_all(
            jnp.repeat(send_rows, 2, axis=0), "ep", split_axis=0, concat_axis=0, tiled=True
        )
        block_out = expert_block(arrived.reshape(-1, model_width), w_gate, w_up, w_down)
        returned = lax.all_to_all(
            block_out.reshape(ep_count, capacity, model_width),
            "ep",
            split_axis=0,
            concat_axis=0,
            tiled=True,
        )
        partial_tokens = combine_rows(
            returned, target, group_weight, group_size, top_count, slot_count, capacity, model_width
        )
        token_out = lax.psum_scatter(partial_tokens, "dp", scatter_dimension=0, tiled=True)
        outputs.append(token_out.astype(jnp.bfloat16))
        load_rows.append(jnp.sum(arrived_counts).reshape(1))
    return (jnp.stack(outputs), jnp.stack(load_rows))


def moe_kernel(
    chunks,
    tok_ref,
    rw_ref,
    ids_ref,
    rep_ref,
    place_ref,
    w_gate_ref,
    w_up_ref,
    w_down_ref,
    out_ref,
    count_ref,
    rw,
    ids,
    rep,
    place,
    wgu,
    wd,
    zbuf,
    gx,
    ps,
    qs,
    qr,
    tbuf,
    zr,
    part_count,
    other_count,
    wsem,
    ssem,
    rsem,
):
    ep, dp = lax.axis_index("ep"), lax.axis_index("dp")
    z, y = ep // 2, ep % 2
    x, c = dp // 2, dp % 2
    steps, width = tok_ref.shape
    hid = w_gate_ref.shape[2]
    part = width // chunks
    block = 4 * steps
    total = 4 * block
    f32, bf16 = jnp.float32, jnp.bfloat16

    def columns(n, more=0):
        return pl.ds(n * part, part + more)

    def load(src, dst, n):
        copy = pltpu.make_async_copy(src, dst, wsem.at[n])
        copy.start()
        return copy

    small = [
        load(src, dst, n)
        for n, (src, dst) in enumerate(
            [(rw_ref, rw), (ids_ref, ids), (rep_ref, rep), (place_ref, place)]
        )
    ]
    own = [
        load(tok_ref.at[:, columns(n)], zbuf.at[n, 0, :, pl.ds(0, part)], 4 + n)
        for n in range(chunks)
    ]
    weights = [
        load(w_gate_ref.at[0], wgu.at[:, pl.ds(0, hid)], 4 + chunks),
        load(w_up_ref.at[0], wgu.at[:, pl.ds(hid, hid)], 5 + chunks),
        load(w_down_ref.at[0], wd.at[pl.ds(0, hid)], 6 + chunks),
    ]

    def device(zz, yy, xx, cc):
        return (zz * 2 + yy, xx * 2 + cc)

    z_others = [z + 1 - 2 * (z % 2), (z + 2) % 4, 3 - z]
    z_dev = [device(zz, y, x, c) for zz in z_others]
    core_dev = device(z, y, x, 1 - c)
    x_dev = device(z, y, 1 - x, c)
    y_dev = device(z, 1 - y, x, c)
    far_dev = device(z, 1 - y, 1 - x, c)
    plane = [(3, far_dev), (2, x_dev), (1, y_dev)]

    barrier = pltpu.get_barrier_semaphore()
    partners = z_dev + [core_dev, x_dev, y_dev, far_dev]
    for partner in partners:
        pl.semaphore_signal(barrier, inc=1, device_id=partner, device_id_type=MESH)

    started = []

    def send(src, dst, to):
        n = len(started)
        copy = pltpu.make_async_remote_copy(
            src_ref=src,
            dst_ref=dst,
            send_sem=ssem.at[n],
            recv_sem=rsem.at[n],
            device_id=to,
            device_id_type=MESH,
        )
        copy.start()
        started.append(copy)
        return copy

    for copy in small:
        copy.wait()
    lane = lax.broadcasted_iota(jnp.int32, (steps, LANES), 1)
    diagonal = lax.broadcasted_iota(jnp.int32, (steps, steps), 0) == lax.broadcasted_iota(
        jnp.int32, (steps, steps), 1
    )
    slots = jnp.zeros(ids.shape, jnp.int32)
    for e in range(place.shape[1]):
        chosen = jnp.where(rep[...] == 0, place[0:1, e : e + 1], place[1:2, e : e + 1])
        slots = slots + jnp.where(ids[...] == e, chosen, 0)
    packed = jnp.zeros((steps, LANES), f32)
    for k in range(ids.shape[0]):
        slot = jnp.sum(jnp.where(diagonal, slots[k : k + 1], 0), axis=1, keepdims=True)
        gain = rw[k : k + 1].astype(f32)
        gain = jnp.sum(jnp.where(diagonal, gain, 0.0), axis=1, keepdims=True)
        packed = packed + jnp.where(lane == slot, gain, 0.0)
        packed = packed + jnp.where(lane == slot + 4, 1.0, 0.0)
    zbuf[chunks - 1, 0, :, part:] = packed.astype(bf16)
    for copy in own:
        copy.wait()
    pl.semaphore_wait(barrier, len(partners))

    def wide(n):
        return pl.ds(0, part + (LANES if n == chunks - 1 else 0))

    def span(n):
        return columns(n, LANES if n == chunks - 1 else 0)

    z_in = [
        [
            send(zbuf.at[n, 0, :, wide(n)], zbuf.at[n, k + 1, :, wide(n)], z_dev[k])
            for k in (2, 1, 0)
        ]
        for n in range(chunks)
    ]

    swapped = [
        send(w_gate_ref.at[0], wgu.at[:, pl.ds(2 * hid, hid)], core_dev),
        send(w_up_ref.at[0], wgu.at[:, pl.ds(3 * hid, hid)], core_dev),
        send(w_down_ref.at[0], wd.at[pl.ds(hid, hid)], core_dev),
    ]

    plane_in = {}

    def spread(n):
        for copy in z_in[n]:
            copy.wait_recv()
        end = part + (LANES if n == chunks - 1 else 0)
        gx[0, :, n * part : n * part + end] = jnp.concatenate(
            [zbuf[n, k, :, 0:end] for k in range(4)], axis=0
        )
        here = gx.at[0, :, span(n)]
        plane_in[n] = [send(here, gx.at[i, :, span(n)], to) for i, to in plane]

    def multiply(n, both):
        if n == 0:
            weights[0].wait()
            weights[1].wait()
            swapped[0].wait_recv()
            swapped[1].wait_recv()
        for copy in plane_in[n]:
            copy.wait_recv()
        rows = gx[:, :, n * part : (n + 1) * part].reshape(total, part)
        more = jnp.dot(rows, wgu[n * part : (n + 1) * part], preferred_element_type=f32)
        return more if both is None else both + more

    both = None
    for n in range(chunks):
        spread(n)
    for n in range(chunks):
        both = multiply(n, both)

    hidden = []
    for i in range(2):
        gate, up = both[:, 2 * i * hid : (2 * i + 1) * hid], both[:, (2 * i + 1) * hid : (2 * i + 2) * hid]
        hidden.append((gate / (1.0 + jnp.exp(-gate)) * up).astype(bf16))
    hidden = jnp.concatenate(hidden, axis=1)
    route = gx[:, :, width : width + LANES].reshape(total, LANES).astype(f32)
    lane = lax.broadcasted_iota(jnp.int32, (total, LANES), 1)
    weight = jnp.sum(jnp.where(lane == z, route, 0.0), axis=1, keepdims=True)
    weights[2].wait()
    swapped[2].wait_recv()

    plane_out, z_out = {}, {}

    def down(n):
        held = wd[:, n * part : (n + 1) * part]
        made = jnp.dot(hidden, held, preferred_element_type=f32) * weight
        made = made.reshape(4, block, part)
        plane_out[n] = []
        for i, to in plane:
            qs[n, i - 1] = made[i].astype(bf16)
            plane_out[n].append(send(qs.at[n, i - 1], qr.at[n, i - 1], to))
        ps[n] = made[0]

    def across(n):
        held = ps[n]
        for (i, _), copy in zip(reversed(plane), reversed(plane_out[n])):
            copy.wait_recv()
            held = held + qr[n, i - 1].astype(f32)
        held = held.astype(bf16)
        for k in range(4):
            tbuf[n, k] = held[k * steps : (k + 1) * steps]
        z_out[n] = [send(tbuf.at[n, k + 1], zr.at[n, k], z_dev[k]) for k in (2, 1, 0)]

    def finish(n):
        final = tbuf[n, 0].astype(f32)
        for copy in z_out[n]:
            copy.wait_recv()
        for k in range(3):
            final = final + zr[n, k].astype(f32)
        out_ref[:, n * part : (n + 1) * part] = final.astype(out_ref.dtype)

    for n in range(chunks):
        down(n)
    counted = jnp.sum(jnp.where(lane == z + 4, route, 0.0), axis=1, keepdims=True)
    row = lax.broadcasted_iota(jnp.int32, (total, LANES), 0)
    per_step = jnp.where(lane == row % steps, counted, 0.0)
    per_step = jnp.sum(per_step, axis=0, keepdims=True)
    part_count[...] = jnp.broadcast_to(per_step, part_count.shape)
    count_in = send(part_count, other_count, core_dev)
    for n in range(chunks):
        across(n)
    count_in.wait_recv()
    count_ref[...] = (part_count[...] + other_count[...])[0:1, :steps].astype(jnp.int32)
    for n in range(chunks):
        finish(n)
    for copy in started:
        copy.wait_send()


def local_gathered(tokens, route_weight, expert_ids, replica, placement, w_gate, w_up, w_down):
    steps, own, width = tokens.shape
    hid = w_gate.shape[2]
    top = expert_ids.shape[2]
    chunks = 2
    part = width // chunks
    block = 4 * steps
    bf16, f32, i32 = jnp.bfloat16, jnp.float32, jnp.int32
    vmem = pl.BlockSpec(memory_space=pltpu.VMEM)
    anywhere = pl.BlockSpec(memory_space=pl.ANY)
    out, count = pl.pallas_call(
        functools.partial(moe_kernel, chunks),
        out_shape=(
            jax.ShapeDtypeStruct((steps, width), bf16),
            jax.ShapeDtypeStruct((1, steps), i32),
        ),
        in_specs=[anywhere] * 8,
        out_specs=(vmem, vmem),
        scratch_shapes=[
            pltpu.VMEM((top, steps), bf16),
            pltpu.VMEM((top, steps), i32),
            pltpu.VMEM((top, steps), i32),
            pltpu.VMEM((2, placement.shape[0]), i32),
            pltpu.VMEM((width, 4 * hid), bf16),
            pltpu.VMEM((2 * hid, width), bf16),
            pltpu.VMEM((chunks, 4, steps, part + LANES), bf16),
            pltpu.VMEM((4, block, width + LANES), bf16),
            pltpu.VMEM((chunks, block, part), f32),
            pltpu.VMEM((chunks, 3, block, part), bf16),
            pltpu.VMEM((chunks, 3, block, part), bf16),
            pltpu.VMEM((chunks, 4, steps, part), bf16),
            pltpu.VMEM((chunks, 3, steps, part), bf16),
            pltpu.VMEM((8, LANES), f32),
            pltpu.VMEM((8, LANES), f32),
            pltpu.SemaphoreType.DMA((7 + chunks,)),
            pltpu.SemaphoreType.DMA((12 * chunks + 4,)),
            pltpu.SemaphoreType.DMA((12 * chunks + 4,)),
        ],
        compiler_params=pltpu.CompilerParams(
            collective_id=0, has_side_effects=True, vmem_limit_bytes=VMEM_LIMIT
        ),
    )(
        tokens.reshape(steps, width),
        route_weight.reshape(steps, top).T,
        expert_ids.reshape(steps, top).T,
        replica.reshape(steps, top).T,
        placement.T,
        w_gate,
        w_up,
        w_down,
    )
    return out.reshape(steps, own, width), count.reshape(steps, 1)


def solution(mesh):
    dense = mesh.shape["ep"] == 8 and mesh.shape["dp"] == 4
    return jax.shard_map(
        local_gathered if dense else local_packed,
        mesh=mesh,
        in_specs=(
            P(None, ("ep", "dp"), None),
            P(None, ("ep", "dp"), None),
            P(None, ("ep", "dp"), None),
            P(None, ("ep", "dp"), None),
            P(),
            P("ep", None, "dp"),
            P("ep", None, "dp"),
            P("ep", "dp", None),
        ),
        out_specs=(P(None, ("ep", "dp"), None), P(None, "ep")),
        check_vma=False,
    )
```

```python
import functools

import jax
import jax.numpy as jnp
from jax import lax
from jax.experimental import pallas as pl
from jax.experimental.pallas import tpu as pltpu
from jax.sharding import PartitionSpec as P

MESH = pl.DeviceIdType.MESH
LANES = 128
VMEM_LIMIT = 60 * 1024 * 1024


def pick_slots(expert_ids, replica, placement):
    logical = placement.shape[0]
    chosen = jnp.where(replica[..., None] == 0, placement[:, 0], placement[:, 1])
    matches = expert_ids[..., None] == jnp.arange(logical, dtype=jnp.int32)
    return jnp.sum(jnp.where(matches, chosen, 0), axis=-1)


def place_rows(group_slots, slot_count):
    flat_slots = group_slots.reshape(-1)
    matches = (flat_slots[:, None] == jnp.arange(slot_count, dtype=jnp.int32)[None, :]).astype(
        jnp.int32
    )
    earlier = jnp.cumsum(matches, axis=0) - matches
    position = jnp.sum(earlier * matches, axis=1)
    counts = jnp.sum(matches, axis=0)
    return (position.reshape(group_slots.shape), counts)


def pack_rows(rows, slots, slot_count, capacity, top_count):
    position, counts = place_rows(slots, slot_count)
    target = (slots * capacity + position).reshape(-1)
    repeated = jnp.repeat(rows, top_count, axis=0)
    packed = jnp.zeros((slot_count * capacity, rows.shape[1]), rows.dtype).at[target].set(repeated)
    return (packed.reshape(slot_count, capacity, rows.shape[1]), target)


def expert_block(expert_rows, w_gate, w_up, w_down):
    gate_out = jnp.dot(expert_rows, w_gate[0], preferred_element_type=jnp.float32)
    up_out = jnp.dot(expert_rows, w_up[0], preferred_element_type=jnp.float32)
    hidden = (jax.nn.silu(gate_out) * up_out).astype(jnp.bfloat16)
    return jnp.dot(hidden, w_down[0], preferred_element_type=jnp.float32).astype(jnp.bfloat16)


def combine_rows(
    returned, target, weight_rows, row_count, top_count, slot_count, capacity, model_width
):
    paired = returned.reshape(slot_count, 2, capacity, model_width)
    first_half = paired[:, 0].reshape(-1, model_width)[target].astype(jnp.float32)
    second_half = paired[:, 1].reshape(-1, model_width)[target].astype(jnp.float32)
    weighted = (first_half + second_half) * weight_rows.reshape(-1, 1).astype(jnp.float32)
    return jnp.sum(weighted.reshape(row_count, top_count, model_width), axis=1)


def local_packed(tokens, route_weight, expert_ids, replica, placement, w_gate, w_up, w_down):
    steps_total = tokens.shape[0]
    model_width = tokens.shape[2]
    ep_count = lax.axis_size("ep")
    dp_count = lax.axis_size("dp")
    slot_count = ep_count // 2
    logical = placement.shape[0]
    top_count = expert_ids.shape[2]
    own_count = expert_ids.shape[1]
    group_size = own_count * dp_count
    capacity = 2 * ((group_size * top_count + logical) // (2 * logical)) + 2
    own_slots = pick_slots(expert_ids, replica, placement)
    outputs = []
    load_rows = []
    for step_index in range(steps_total):
        group_slots = lax.all_gather(own_slots[step_index], "dp", axis=0, tiled=True)
        group_counts = place_rows(group_slots, slot_count)[1]
        arrived_counts = lax.all_to_all(
            jnp.repeat(group_counts, 2), "ep", split_axis=0, concat_axis=0, tiled=True
        )
        grouped, group_weight = (
            lax.all_gather(tokens[step_index], "dp", axis=0, tiled=True),
            lax.all_gather(route_weight[step_index], "dp", axis=0, tiled=True),
        )
        send_rows, target = pack_rows(grouped, group_slots, slot_count, capacity, top_count)
        arrived = lax.all_to_all(
            jnp.repeat(send_rows, 2, axis=0), "ep", split_axis=0, concat_axis=0, tiled=True
        )
        block_out = expert_block(arrived.reshape(-1, model_width), w_gate, w_up, w_down)
        returned = lax.all_to_all(
            block_out.reshape(ep_count, capacity, model_width),
            "ep",
            split_axis=0,
            concat_axis=0,
            tiled=True,
        )
        partial_tokens = combine_rows(
            returned, target, group_weight, group_size, top_count, slot_count, capacity, model_width
        )
        token_out = lax.psum_scatter(partial_tokens, "dp", scatter_dimension=0, tiled=True)
        outputs.append(token_out.astype(jnp.bfloat16))
        load_rows.append(jnp.sum(arrived_counts).reshape(1))
    return (jnp.stack(outputs), jnp.stack(load_rows))


def moe_kernel(
    chunks,
    tok_ref,
    rw_ref,
    ids_ref,
    rep_ref,
    place_ref,
    w_gate_ref,
    w_up_ref,
    w_down_ref,
    out_ref,
    count_ref,
    rw,
    ids,
    rep,
    place,
    wgu,
    wd,
    zbuf,
    gx,
    ps,
    qs,
    qr,
    tbuf,
    zr,
    part_count,
    other_count,
    wsem,
    ssem,
    rsem,
):
    ep, dp = lax.axis_index("ep"), lax.axis_index("dp")
    z, y = ep // 2, ep % 2
    x, c = dp // 2, dp % 2
    steps, width = tok_ref.shape
    hid = w_gate_ref.shape[2]
    part = width // chunks
    block = 4 * steps
    total = 4 * block
    f32, bf16 = jnp.float32, jnp.bfloat16

    def columns(n, more=0):
        return pl.ds(n * part, part + more)

    def load(src, dst, n):
        copy = pltpu.make_async_copy(src, dst, wsem.at[n])
        copy.start()
        return copy

    small = [
        load(src, dst, n)
        for n, (src, dst) in enumerate(
            [(rw_ref, rw), (ids_ref, ids), (rep_ref, rep), (place_ref, place)]
        )
    ]
    own = [
        load(tok_ref.at[:, columns(n)], zbuf.at[n, 0, :, pl.ds(0, part)], 4 + n)
        for n in range(chunks)
    ]
    weights = [
        load(w_gate_ref.at[0], wgu.at[:, pl.ds(0, hid)], 4 + chunks),
        load(w_up_ref.at[0], wgu.at[:, pl.ds(hid, hid)], 5 + chunks),
        load(w_down_ref.at[0], wd.at[pl.ds(0, hid)], 6 + chunks),
    ]

    def device(zz, yy, xx, cc):
        return (zz * 2 + yy, xx * 2 + cc)

    z_others = [z + 1 - 2 * (z % 2), (z + 2) % 4, 3 - z]
    z_dev = [device(zz, y, x, c) for zz in z_others]
    core_dev = device(z, y, x, 1 - c)
    x_dev = device(z, y, 1 - x, c)
    y_dev = device(z, 1 - y, x, c)
    far_dev = device(z, 1 - y, 1 - x, c)
    plane = [(3, far_dev), (2, x_dev), (1, y_dev)]

    barrier = pltpu.get_barrier_semaphore()
    partners = z_dev + [core_dev, x_dev, y_dev, far_dev]
    for partner in partners:
        pl.semaphore_signal(barrier, inc=1, device_id=partner, device_id_type=MESH)

    started = []

    def send(src, dst, to):
        n = len(started)
        copy = pltpu.make_async_remote_copy(
            src_ref=src,
            dst_ref=dst,
            send_sem=ssem.at[n],
            recv_sem=rsem.at[n],
            device_id=to,
            device_id_type=MESH,
        )
        copy.start()
        started.append(copy)
        return copy

    for copy in small:
        copy.wait()
    lane = lax.broadcasted_iota(jnp.int32, (steps, LANES), 1)
    diagonal = lax.broadcasted_iota(jnp.int32, (steps, steps), 0) == lax.broadcasted_iota(
        jnp.int32, (steps, steps), 1
    )
    slots = jnp.zeros(ids.shape, jnp.int32)
    for e in range(place.shape[1]):
        chosen = jnp.where(rep[...] == 0, place[0:1, e : e + 1], place[1:2, e : e + 1])
        slots = slots + jnp.where(ids[...] == e, chosen, 0)
    packed = jnp.zeros((steps, LANES), f32)
    for k in range(ids.shape[0]):
        slot = jnp.sum(jnp.where(diagonal, slots[k : k + 1], 0), axis=1, keepdims=True)
        gain = rw[k : k + 1].astype(f32)
        gain = jnp.sum(jnp.where(diagonal, gain, 0.0), axis=1, keepdims=True)
        packed = packed + jnp.where(lane == slot, gain, 0.0)
        packed = packed + jnp.where(lane == slot + 4, 1.0, 0.0)
    zbuf[chunks - 1, 0, :, part:] = packed.astype(bf16)
    for copy in own:
        copy.wait()
    pl.semaphore_wait(barrier, len(partners))

    def wide(n):
        return pl.ds(0, part + (LANES if n == chunks - 1 else 0))

    def span(n):
        return columns(n, LANES if n == chunks - 1 else 0)

    z_in = [
        [
            send(zbuf.at[n, 0, :, wide(n)], zbuf.at[n, k + 1, :, wide(n)], z_dev[k])
            for k in (2, 1, 0)
        ]
        for n in range(chunks)
    ]

    swapped = [
        send(w_gate_ref.at[0], wgu.at[:, pl.ds(2 * hid, hid)], core_dev),
        send(w_up_ref.at[0], wgu.at[:, pl.ds(3 * hid, hid)], core_dev),
        send(w_down_ref.at[0], wd.at[pl.ds(hid, hid)], core_dev),
    ]

    plane_in = {}

    def spread(n):
        for copy in z_in[n]:
            copy.wait_recv()
        end = part + (LANES if n == chunks - 1 else 0)
        gx[0, :, n * part : n * part + end] = jnp.concatenate(
            [zbuf[n, k, :, 0:end] for k in range(4)], axis=0
        )
        here = gx.at[0, :, span(n)]
        plane_in[n] = [send(here, gx.at[i, :, span(n)], to) for i, to in plane]

    def multiply(n, both):
        if n == 0:
            weights[0].wait()
            weights[1].wait()
            swapped[0].wait_recv()
            swapped[1].wait_recv()
        for copy in plane_in[n]:
            copy.wait_recv()
        rows = gx[:, :, n * part : (n + 1) * part].reshape(total, part)
        more = jnp.dot(rows, wgu[n * part : (n + 1) * part], preferred_element_type=f32)
        return more if both is None else both + more

    both = None
    for n in range(chunks):
        spread(n)
    for n in range(chunks):
        both = multiply(n, both)

    hidden = []
    for i in range(2):
        gate, up = both[:, 2 * i * hid : (2 * i + 1) * hid], both[:, (2 * i + 1) * hid : (2 * i + 2) * hid]
        hidden.append((gate / (1.0 + jnp.exp(-gate)) * up).astype(bf16))
    hidden = jnp.concatenate(hidden, axis=1)
    route = gx[:, :, width : width + LANES].reshape(total, LANES).astype(f32)
    lane = lax.broadcasted_iota(jnp.int32, (total, LANES), 1)
    weight = jnp.sum(jnp.where(lane == z, route, 0.0), axis=1, keepdims=True)
    weights[2].wait()
    swapped[2].wait_recv()

    plane_out, z_out = {}, {}

    def down(n):
        held = wd[:, n * part : (n + 1) * part]
        made = jnp.dot(hidden, held, preferred_element_type=f32) * weight
        made = made.reshape(4, block, part)
        plane_out[n] = []
        for i, to in plane:
            qs[n, i - 1] = made[i].astype(bf16)
            plane_out[n].append(send(qs.at[n, i - 1], qr.at[n, i - 1], to))
        ps[n] = made[0]

    def across(n):
        held = ps[n]
        for (i, _), copy in zip(reversed(plane), reversed(plane_out[n])):
            copy.wait_recv()
            held = held + qr[n, i - 1].astype(f32)
        held = held.astype(bf16)
        for k in range(4):
            tbuf[n, k] = held[k * steps : (k + 1) * steps]
        z_out[n] = [send(tbuf.at[n, k + 1], zr.at[n, k], z_dev[k]) for k in (2, 1, 0)]

    def finish(n):
        final = tbuf[n, 0].astype(f32)
        for copy in z_out[n]:
            copy.wait_recv()
        for k in range(3):
            final = final + zr[n, k].astype(f32)
        out_ref[:, n * part : (n + 1) * part] = final.astype(out_ref.dtype)

    for n in range(chunks):
        down(n)
    counted = jnp.sum(jnp.where(lane == z + 4, route, 0.0), axis=1, keepdims=True)
    row = lax.broadcasted_iota(jnp.int32, (total, LANES), 0)
    per_step = jnp.where(lane == row % steps, counted, 0.0)
    per_step = jnp.sum(per_step, axis=0, keepdims=True)
    part_count[...] = jnp.broadcast_to(per_step, part_count.shape)
    count_in = send(part_count, other_count, core_dev)
    for n in range(chunks):
        across(n)
    count_in.wait_recv()
    count_ref[...] = (part_count[...] + other_count[...])[0:1, :steps].astype(jnp.int32)
    for n in range(chunks):
        finish(n)
    for copy in started:
        copy.wait_send()


def hand_over(made_ref, made_count_ref, out_ref, count_ref, sem):
    copies = [
        pltpu.make_async_copy(made_ref, out_ref, sem.at[0]),
        pltpu.make_async_copy(made_count_ref, count_ref, sem.at[1]),
    ]
    for copy in copies:
        copy.start()
    for copy in copies:
        copy.wait()


def local_gathered(tokens, route_weight, expert_ids, replica, placement, w_gate, w_up, w_down):
    steps, own, width = tokens.shape
    hid = w_gate.shape[2]
    top = expert_ids.shape[2]
    chunks = 2
    part = width // chunks
    block = 4 * steps
    bf16, f32, i32 = jnp.bfloat16, jnp.float32, jnp.int32
    vmem = pl.BlockSpec(memory_space=pltpu.VMEM)
    anywhere = pl.BlockSpec(memory_space=pl.ANY)
    out, count = pl.pallas_call(
        functools.partial(moe_kernel, chunks),
        out_shape=(
            jax.ShapeDtypeStruct((steps, width), bf16),
            jax.ShapeDtypeStruct((1, steps), i32),
        ),
        in_specs=[anywhere] * 8,
        out_specs=(vmem, vmem),
        scratch_shapes=[
            pltpu.VMEM((top, steps), bf16),
            pltpu.VMEM((top, steps), i32),
            pltpu.VMEM((top, steps), i32),
            pltpu.VMEM((2, placement.shape[0]), i32),
            pltpu.VMEM((width, 4 * hid), bf16),
            pltpu.VMEM((2 * hid, width), bf16),
            pltpu.VMEM((chunks, 4, steps, part + LANES), bf16),
            pltpu.VMEM((4, block, width + LANES), bf16),
            pltpu.VMEM((chunks, block, part), f32),
            pltpu.VMEM((chunks, 3, block, part), bf16),
            pltpu.VMEM((chunks, 3, block, part), bf16),
            pltpu.VMEM((chunks, 4, steps, part), bf16),
            pltpu.VMEM((chunks, 3, steps, part), bf16),
            pltpu.VMEM((8, LANES), f32),
            pltpu.VMEM((8, LANES), f32),
            pltpu.SemaphoreType.DMA((7 + chunks,)),
            pltpu.SemaphoreType.DMA((12 * chunks + 4,)),
            pltpu.SemaphoreType.DMA((12 * chunks + 4,)),
        ],
        compiler_params=pltpu.CompilerParams(
            collective_id=0, has_side_effects=True, vmem_limit_bytes=VMEM_LIMIT
        ),
    )(
        tokens.reshape(steps, width),
        route_weight.reshape(steps, top).T,
        expert_ids.reshape(steps, top).T,
        replica.reshape(steps, top).T,
        placement.T,
        w_gate,
        w_up,
        w_down,
    )
    out, count = pl.pallas_call(
        hand_over,
        out_shape=(
            jax.ShapeDtypeStruct(out.shape, out.dtype),
            jax.ShapeDtypeStruct(count.shape, count.dtype),
        ),
        in_specs=[anywhere] * 2,
        out_specs=(anywhere, anywhere),
        scratch_shapes=[pltpu.SemaphoreType.DMA((2,))],
        compiler_params=pltpu.CompilerParams(vmem_limit_bytes=VMEM_LIMIT),
    )(out, count)
    return out.reshape(steps, own, width), count.reshape(steps, 1)


def solution(mesh):
    dense = mesh.shape["ep"] == 8 and mesh.shape["dp"] == 4
    return jax.shard_map(
        local_gathered if dense else local_packed,
        mesh=mesh,
        in_specs=(
            P(None, ("ep", "dp"), None),
            P(None, ("ep", "dp"), None),
            P(None, ("ep", "dp"), None),
            P(None, ("ep", "dp"), None),
            P(),
            P("ep", None, "dp"),
            P("ep", None, "dp"),
            P("ep", "dp", None),
        ),
        out_specs=(P(None, ("ep", "dp"), None), P(None, "ep")),
        check_vma=False,
    )
```

```python
import functools

import jax
import jax.numpy as jnp
from jax import lax
from jax.experimental import pallas as pl
from jax.experimental.pallas import tpu as pltpu
from jax.sharding import PartitionSpec as P

MESH = pl.DeviceIdType.MESH
LANES = 128
VMEM_LIMIT = 60 * 1024 * 1024


def pick_slots(expert_ids, replica, placement):
    logical = placement.shape[0]
    chosen = jnp.where(replica[..., None] == 0, placement[:, 0], placement[:, 1])
    matches = expert_ids[..., None] == jnp.arange(logical, dtype=jnp.int32)
    return jnp.sum(jnp.where(matches, chosen, 0), axis=-1)


def place_rows(group_slots, slot_count):
    flat_slots = group_slots.reshape(-1)
    matches = (flat_slots[:, None] == jnp.arange(slot_count, dtype=jnp.int32)[None, :]).astype(
        jnp.int32
    )
    earlier = jnp.cumsum(matches, axis=0) - matches
    position = jnp.sum(earlier * matches, axis=1)
    counts = jnp.sum(matches, axis=0)
    return (position.reshape(group_slots.shape), counts)


def pack_rows(rows, slots, slot_count, capacity, top_count):
    position, counts = place_rows(slots, slot_count)
    target = (slots * capacity + position).reshape(-1)
    repeated = jnp.repeat(rows, top_count, axis=0)
    packed = jnp.zeros((slot_count * capacity, rows.shape[1]), rows.dtype).at[target].set(repeated)
    return (packed.reshape(slot_count, capacity, rows.shape[1]), target)


def expert_block(expert_rows, w_gate, w_up, w_down):
    gate_out = jnp.dot(expert_rows, w_gate[0], preferred_element_type=jnp.float32)
    up_out = jnp.dot(expert_rows, w_up[0], preferred_element_type=jnp.float32)
    hidden = (jax.nn.silu(gate_out) * up_out).astype(jnp.bfloat16)
    return jnp.dot(hidden, w_down[0], preferred_element_type=jnp.float32).astype(jnp.bfloat16)


def combine_rows(
    returned, target, weight_rows, row_count, top_count, slot_count, capacity, model_width
):
    paired = returned.reshape(slot_count, 2, capacity, model_width)
    first_half = paired[:, 0].reshape(-1, model_width)[target].astype(jnp.float32)
    second_half = paired[:, 1].reshape(-1, model_width)[target].astype(jnp.float32)
    weighted = (first_half + second_half) * weight_rows.reshape(-1, 1).astype(jnp.float32)
    return jnp.sum(weighted.reshape(row_count, top_count, model_width), axis=1)


def local_packed(tokens, route_weight, expert_ids, replica, placement, w_gate, w_up, w_down):
    steps_total = tokens.shape[0]
    model_width = tokens.shape[2]
    ep_count = lax.axis_size("ep")
    dp_count = lax.axis_size("dp")
    slot_count = ep_count // 2
    logical = placement.shape[0]
    top_count = expert_ids.shape[2]
    own_count = expert_ids.shape[1]
    group_size = own_count * dp_count
    capacity = 2 * ((group_size * top_count + logical) // (2 * logical)) + 2
    own_slots = pick_slots(expert_ids, replica, placement)
    outputs = []
    load_rows = []
    for step_index in range(steps_total):
        group_slots = lax.all_gather(own_slots[step_index], "dp", axis=0, tiled=True)
        group_counts = place_rows(group_slots, slot_count)[1]
        arrived_counts = lax.all_to_all(
            jnp.repeat(group_counts, 2), "ep", split_axis=0, concat_axis=0, tiled=True
        )
        grouped, group_weight = (
            lax.all_gather(tokens[step_index], "dp", axis=0, tiled=True),
            lax.all_gather(route_weight[step_index], "dp", axis=0, tiled=True),
        )
        send_rows, target = pack_rows(grouped, group_slots, slot_count, capacity, top_count)
        arrived = lax.all_to_all(
            jnp.repeat(send_rows, 2, axis=0), "ep", split_axis=0, concat_axis=0, tiled=True
        )
        block_out = expert_block(arrived.reshape(-1, model_width), w_gate, w_up, w_down)
        returned = lax.all_to_all(
            block_out.reshape(ep_count, capacity, model_width),
            "ep",
            split_axis=0,
            concat_axis=0,
            tiled=True,
        )
        partial_tokens = combine_rows(
            returned, target, group_weight, group_size, top_count, slot_count, capacity, model_width
        )
        token_out = lax.psum_scatter(partial_tokens, "dp", scatter_dimension=0, tiled=True)
        outputs.append(token_out.astype(jnp.bfloat16))
        load_rows.append(jnp.sum(arrived_counts).reshape(1))
    return (jnp.stack(outputs), jnp.stack(load_rows))


def moe_kernel(
    tiles,
    tok_ref,
    rw_ref,
    ids_ref,
    rep_ref,
    place_ref,
    w_gate_ref,
    w_up_ref,
    w_down_ref,
    out_ref,
    count_ref,
    rw,
    ids,
    rep,
    place,
    wgu,
    wd,
    zbuf,
    gx,
    ps,
    qs,
    qr,
    tbuf,
    zr,
    part_count,
    other_count,
    wsem,
    ssem,
    rsem,
):
    ep, dp = lax.axis_index("ep"), lax.axis_index("dp")
    z, y = ep // 2, ep % 2
    x, c = dp // 2, dp % 2
    steps, width = tok_ref.shape
    hid = w_gate_ref.shape[2]
    chunks = len(tiles)
    edges = [sum(tiles[:n]) * LANES for n in range(chunks + 1)]
    ends = edges[1:chunks] + [width + LANES]
    block = 4 * steps
    total = 4 * block
    f32, bf16 = jnp.float32, jnp.bfloat16

    def columns(n):
        return pl.ds(edges[n], edges[n + 1] - edges[n])

    def span(n):
        return pl.ds(edges[n], ends[n] - edges[n])

    def load(src, dst, n):
        copy = pltpu.make_async_copy(src, dst, wsem.at[n])
        copy.start()
        return copy

    small = [
        load(src, dst, n)
        for n, (src, dst) in enumerate(
            [(rw_ref, rw), (ids_ref, ids), (rep_ref, rep), (place_ref, place)]
        )
    ]
    own = [
        load(tok_ref.at[:, columns(n)], zbuf.at[0, :, columns(n)], 4 + n)
        for n in range(chunks)
    ]
    weights = [
        load(w_gate_ref.at[0], wgu.at[:, pl.ds(0, hid)], 4 + chunks),
        load(w_up_ref.at[0], wgu.at[:, pl.ds(hid, hid)], 5 + chunks),
        load(w_down_ref.at[0], wd.at[pl.ds(0, hid)], 6 + chunks),
    ]

    def device(zz, yy, xx, cc):
        return (zz * 2 + yy, xx * 2 + cc)

    z_others = [z + 1 - 2 * (z % 2), (z + 2) % 4, 3 - z]
    z_dev = [device(zz, y, x, c) for zz in z_others]
    core_dev = device(z, y, x, 1 - c)
    x_dev = device(z, y, 1 - x, c)
    y_dev = device(z, 1 - y, x, c)
    far_dev = device(z, 1 - y, 1 - x, c)
    plane = [(3, far_dev), (2, x_dev), (1, y_dev)]

    barrier = pltpu.get_barrier_semaphore()
    partners = z_dev + [core_dev, x_dev, y_dev, far_dev]
    for partner in partners:
        pl.semaphore_signal(barrier, inc=1, device_id=partner, device_id_type=MESH)

    started = []

    def send(src, dst, to):
        n = len(started)
        copy = pltpu.make_async_remote_copy(
            src_ref=src,
            dst_ref=dst,
            send_sem=ssem.at[n],
            recv_sem=rsem.at[n],
            device_id=to,
            device_id_type=MESH,
        )
        copy.start()
        started.append(copy)
        return copy

    for copy in small:
        copy.wait()
    lane = lax.broadcasted_iota(jnp.int32, (steps, LANES), 1)
    diagonal = lax.broadcasted_iota(jnp.int32, (steps, steps), 0) == lax.broadcasted_iota(
        jnp.int32, (steps, steps), 1
    )
    slots = jnp.zeros(ids.shape, jnp.int32)
    for e in range(place.shape[1]):
        chosen = jnp.where(rep[...] == 0, place[0:1, e : e + 1], place[1:2, e : e + 1])
        slots = slots + jnp.where(ids[...] == e, chosen, 0)
    packed = jnp.zeros((steps, LANES), f32)
    for k in range(ids.shape[0]):
        slot = jnp.sum(jnp.where(diagonal, slots[k : k + 1], 0), axis=1, keepdims=True)
        gain = rw[k : k + 1].astype(f32)
        gain = jnp.sum(jnp.where(diagonal, gain, 0.0), axis=1, keepdims=True)
        packed = packed + jnp.where(lane == slot, gain, 0.0)
        packed = packed + jnp.where(lane == slot + 4, 1.0, 0.0)
    zbuf[0, :, width:] = packed.astype(bf16)
    for copy in own:
        copy.wait()
    pl.semaphore_wait(barrier, len(partners))

    z_in = [
        [
            send(zbuf.at[0, :, span(n)], zbuf.at[k + 1, :, span(n)], z_dev[k])
            for k in (2, 1, 0)
        ]
        for n in range(chunks)
    ]

    swapped = [
        send(w_gate_ref.at[0], wgu.at[:, pl.ds(2 * hid, hid)], core_dev),
        send(w_up_ref.at[0], wgu.at[:, pl.ds(3 * hid, hid)], core_dev),
        send(w_down_ref.at[0], wd.at[pl.ds(hid, hid)], core_dev),
    ]

    plane_in = {}

    def spread(n):
        for copy in z_in[n]:
            copy.wait_recv()
        lo, hi = edges[n], ends[n]
        gx[0, :, lo:hi] = jnp.concatenate([zbuf[k, :, lo:hi] for k in range(4)], axis=0)
        here = gx.at[0, :, span(n)]
        plane_in[n] = [send(here, gx.at[i, :, span(n)], to) for i, to in plane]

    def multiply(n, both):
        if n == 0:
            weights[0].wait()
            weights[1].wait()
            swapped[0].wait_recv()
            swapped[1].wait_recv()
        for copy in plane_in[n]:
            copy.wait_recv()
        lo, hi = edges[n], edges[n + 1]
        rows = gx[:, :, lo:hi].reshape(total, hi - lo)
        more = jnp.dot(rows, wgu[lo:hi], preferred_element_type=f32)
        return more if both is None else both + more

    both = None
    for n in range(chunks):
        spread(n)
    for n in range(chunks):
        both = multiply(n, both)

    hidden = []
    for i in range(2):
        gate, up = both[:, 2 * i * hid : (2 * i + 1) * hid], both[:, (2 * i + 1) * hid : (2 * i + 2) * hid]
        hidden.append((gate / (1.0 + jnp.exp(-gate)) * up).astype(bf16))
    hidden = jnp.concatenate(hidden, axis=1)
    route = gx[:, :, width : width + LANES].reshape(total, LANES).astype(f32)
    lane = lax.broadcasted_iota(jnp.int32, (total, LANES), 1)
    weight = jnp.sum(jnp.where(lane == z, route, 0.0), axis=1, keepdims=True)
    weights[2].wait()
    swapped[2].wait_recv()

    plane_out, z_out = {}, {}

    def down(n):
        lo, hi = edges[n], edges[n + 1]
        made = jnp.dot(hidden, wd[:, lo:hi], preferred_element_type=f32) * weight
        made = made.reshape(4, block, hi - lo)
        plane_out[n] = []
        for i, to in plane:
            qs[i - 1, :, lo:hi] = made[i].astype(bf16)
            here = qs.at[i - 1, :, columns(n)]
            plane_out[n].append(send(here, qr.at[i - 1, :, columns(n)], to))
        ps[:, lo:hi] = made[0]

    def across(n):
        lo, hi = edges[n], edges[n + 1]
        held = ps[:, lo:hi]
        for (i, _), copy in zip(reversed(plane), reversed(plane_out[n])):
            copy.wait_recv()
            held = held + qr[i - 1, :, lo:hi].astype(f32)
        held = held.astype(bf16)
        for k in range(4):
            tbuf[k, :, lo:hi] = held[k * steps : (k + 1) * steps]
        z_out[n] = [
            send(tbuf.at[k + 1, :, columns(n)], zr.at[k, :, columns(n)], z_dev[k])
            for k in (2, 1, 0)
        ]

    def finish(n):
        lo, hi = edges[n], edges[n + 1]
        final = tbuf[0, :, lo:hi].astype(f32)
        for copy in z_out[n]:
            copy.wait_recv()
        for k in range(3):
            final = final + zr[k, :, lo:hi].astype(f32)
        out_ref[:, lo:hi] = final.astype(out_ref.dtype)

    for n in range(chunks):
        down(n)
    counted = jnp.sum(jnp.where(lane == z + 4, route, 0.0), axis=1, keepdims=True)
    row = lax.broadcasted_iota(jnp.int32, (total, LANES), 0)
    per_step = jnp.where(lane == row % steps, counted, 0.0)
    per_step = jnp.sum(per_step, axis=0, keepdims=True)
    part_count[...] = jnp.broadcast_to(per_step, part_count.shape)
    count_in = send(part_count, other_count, core_dev)
    for n in range(chunks):
        across(n)
    count_in.wait_recv()
    count_ref[...] = (part_count[...] + other_count[...])[0:1, :steps].astype(jnp.int32)
    for n in range(chunks):
        finish(n)
    for copy in started:
        copy.wait_send()


def local_gathered(tokens, route_weight, expert_ids, replica, placement, w_gate, w_up, w_down):
    steps, own, width = tokens.shape
    hid = w_gate.shape[2]
    top = expert_ids.shape[2]
    cols = width // LANES
    tiles = [2 * cols // 7, cols - 2 * (2 * cols // 7), 2 * cols // 7]
    chunks = len(tiles)
    block = 4 * steps
    bf16, f32, i32 = jnp.bfloat16, jnp.float32, jnp.int32
    vmem = pl.BlockSpec(memory_space=pltpu.VMEM)
    anywhere = pl.BlockSpec(memory_space=pl.ANY)
    out, count = pl.pallas_call(
        functools.partial(moe_kernel, tiles),
        out_shape=(
            jax.ShapeDtypeStruct((steps, width), f32),
            jax.ShapeDtypeStruct((1, steps), i32),
        ),
        in_specs=[anywhere] * 8,
        out_specs=(vmem, vmem),
        scratch_shapes=[
            pltpu.VMEM((top, steps), bf16),
            pltpu.VMEM((top, steps), i32),
            pltpu.VMEM((top, steps), i32),
            pltpu.VMEM((2, placement.shape[0]), i32),
            pltpu.VMEM((width, 4 * hid), bf16),
            pltpu.VMEM((2 * hid, width), bf16),
            pltpu.VMEM((4, steps, width + LANES), bf16),
            pltpu.VMEM((4, block, width + LANES), bf16),
            pltpu.VMEM((block, width), f32),
            pltpu.VMEM((3, block, width), bf16),
            pltpu.VMEM((3, block, width), bf16),
            pltpu.VMEM((4, steps, width), bf16),
            pltpu.VMEM((3, steps, width), bf16),
            pltpu.VMEM((8, LANES), f32),
            pltpu.VMEM((8, LANES), f32),
            pltpu.SemaphoreType.DMA((7 + chunks,)),
            pltpu.SemaphoreType.DMA((12 * chunks + 4,)),
            pltpu.SemaphoreType.DMA((12 * chunks + 4,)),
        ],
        compiler_params=pltpu.CompilerParams(
            collective_id=0, has_side_effects=True, vmem_limit_bytes=VMEM_LIMIT
        ),
    )(
        tokens.reshape(steps, width),
        route_weight.reshape(steps, top).T,
        expert_ids.reshape(steps, top).T,
        replica.reshape(steps, top).T,
        placement.T,
        w_gate,
        w_up,
        w_down,
    )
    return out.astype(bf16).reshape(steps, own, width), count.reshape(steps, 1)


def solution(mesh):
    dense = mesh.shape["ep"] == 8 and mesh.shape["dp"] == 4
    return jax.shard_map(
        local_gathered if dense else local_packed,
        mesh=mesh,
        in_specs=(
            P(None, ("ep", "dp"), None),
            P(None, ("ep", "dp"), None),
            P(None, ("ep", "dp"), None),
            P(None, ("ep", "dp"), None),
            P(),
            P("ep", None, "dp"),
            P("ep", None, "dp"),
            P("ep", "dp", None),
        ),
        out_specs=(P(None, ("ep", "dp"), None), P(None, "ep")),
        check_vma=False,
    )
```

```python
import functools

import jax
import jax.numpy as jnp
from jax import lax
from jax.experimental import pallas as pl
from jax.experimental.pallas import tpu as pltpu
from jax.sharding import PartitionSpec as P

MESH = pl.DeviceIdType.MESH
LANES = 128
VMEM_LIMIT = 60 * 1024 * 1024


def pick_slots(expert_ids, replica, placement):
    logical = placement.shape[0]
    chosen = jnp.where(replica[..., None] == 0, placement[:, 0], placement[:, 1])
    matches = expert_ids[..., None] == jnp.arange(logical, dtype=jnp.int32)
    return jnp.sum(jnp.where(matches, chosen, 0), axis=-1)


def place_rows(group_slots, slot_count):
    flat_slots = group_slots.reshape(-1)
    matches = (flat_slots[:, None] == jnp.arange(slot_count, dtype=jnp.int32)[None, :]).astype(
        jnp.int32
    )
    earlier = jnp.cumsum(matches, axis=0) - matches
    position = jnp.sum(earlier * matches, axis=1)
    counts = jnp.sum(matches, axis=0)
    return (position.reshape(group_slots.shape), counts)


def pack_rows(rows, slots, slot_count, capacity, top_count):
    position, counts = place_rows(slots, slot_count)
    target = (slots * capacity + position).reshape(-1)
    repeated = jnp.repeat(rows, top_count, axis=0)
    packed = jnp.zeros((slot_count * capacity, rows.shape[1]), rows.dtype).at[target].set(repeated)
    return (packed.reshape(slot_count, capacity, rows.shape[1]), target)


def expert_block(expert_rows, w_gate, w_up, w_down):
    gate_out = jnp.dot(expert_rows, w_gate[0], preferred_element_type=jnp.float32)
    up_out = jnp.dot(expert_rows, w_up[0], preferred_element_type=jnp.float32)
    hidden = (jax.nn.silu(gate_out) * up_out).astype(jnp.bfloat16)
    return jnp.dot(hidden, w_down[0], preferred_element_type=jnp.float32).astype(jnp.bfloat16)


def combine_rows(
    returned, target, weight_rows, row_count, top_count, slot_count, capacity, model_width
):
    paired = returned.reshape(slot_count, 2, capacity, model_width)
    first_half = paired[:, 0].reshape(-1, model_width)[target].astype(jnp.float32)
    second_half = paired[:, 1].reshape(-1, model_width)[target].astype(jnp.float32)
    weighted = (first_half + second_half) * weight_rows.reshape(-1, 1).astype(jnp.float32)
    return jnp.sum(weighted.reshape(row_count, top_count, model_width), axis=1)


def local_packed(tokens, route_weight, expert_ids, replica, placement, w_gate, w_up, w_down):
    steps_total = tokens.shape[0]
    model_width = tokens.shape[2]
    ep_count = lax.axis_size("ep")
    dp_count = lax.axis_size("dp")
    slot_count = ep_count // 2
    logical = placement.shape[0]
    top_count = expert_ids.shape[2]
    own_count = expert_ids.shape[1]
    group_size = own_count * dp_count
    capacity = 2 * ((group_size * top_count + logical) // (2 * logical)) + 2
    own_slots = pick_slots(expert_ids, replica, placement)
    outputs = []
    load_rows = []
    for step_index in range(steps_total):
        group_slots = lax.all_gather(own_slots[step_index], "dp", axis=0, tiled=True)
        group_counts = place_rows(group_slots, slot_count)[1]
        arrived_counts = lax.all_to_all(
            jnp.repeat(group_counts, 2), "ep", split_axis=0, concat_axis=0, tiled=True
        )
        grouped, group_weight = (
            lax.all_gather(tokens[step_index], "dp", axis=0, tiled=True),
            lax.all_gather(route_weight[step_index], "dp", axis=0, tiled=True),
        )
        send_rows, target = pack_rows(grouped, group_slots, slot_count, capacity, top_count)
        arrived = lax.all_to_all(
            jnp.repeat(send_rows, 2, axis=0), "ep", split_axis=0, concat_axis=0, tiled=True
        )
        block_out = expert_block(arrived.reshape(-1, model_width), w_gate, w_up, w_down)
        returned = lax.all_to_all(
            block_out.reshape(ep_count, capacity, model_width),
            "ep",
            split_axis=0,
            concat_axis=0,
            tiled=True,
        )
        partial_tokens = combine_rows(
            returned, target, group_weight, group_size, top_count, slot_count, capacity, model_width
        )
        token_out = lax.psum_scatter(partial_tokens, "dp", scatter_dimension=0, tiled=True)
        outputs.append(token_out.astype(jnp.bfloat16))
        load_rows.append(jnp.sum(arrived_counts).reshape(1))
    return (jnp.stack(outputs), jnp.stack(load_rows))


def moe_kernel(
    tiles,
    tok_ref,
    rw_ref,
    ids_ref,
    rep_ref,
    place_ref,
    w_gate_ref,
    w_up_ref,
    w_down_ref,
    out_ref,
    count_ref,
    rw,
    ids,
    rep,
    place,
    wgu,
    wd,
    zbuf,
    gx,
    ps,
    qs,
    qr,
    tbuf,
    zr,
    part_count,
    other_count,
    wsem,
    ssem,
    rsem,
):
    ep, dp = lax.axis_index("ep"), lax.axis_index("dp")
    z, y = ep // 2, ep % 2
    x, c = dp // 2, dp % 2
    steps, width = tok_ref.shape
    hid = w_gate_ref.shape[2]
    chunks = len(tiles)
    edges = [sum(tiles[:n]) * LANES for n in range(chunks + 1)]
    ends = edges[1:chunks] + [width + LANES]
    block = 4 * steps
    total = 4 * block
    f32, bf16 = jnp.float32, jnp.bfloat16

    def columns(n):
        return pl.ds(edges[n], edges[n + 1] - edges[n])

    def span(n):
        return pl.ds(edges[n], ends[n] - edges[n])

    def load(src, dst, n):
        copy = pltpu.make_async_copy(src, dst, wsem.at[n])
        copy.start()
        return copy

    small = [
        load(src, dst, n)
        for n, (src, dst) in enumerate(
            [(rw_ref, rw), (ids_ref, ids), (rep_ref, rep), (place_ref, place)]
        )
    ]
    own = [
        load(tok_ref.at[:, columns(n)], zbuf.at[0, :, columns(n)], 4 + n)
        for n in range(chunks)
    ]
    weights = [
        load(w_gate_ref.at[0], wgu.at[:, pl.ds(0, hid)], 4 + chunks),
        load(w_up_ref.at[0], wgu.at[:, pl.ds(hid, hid)], 5 + chunks),
        load(w_down_ref.at[0], wd.at[pl.ds(0, hid)], 6 + chunks),
    ]

    def device(zz, yy, xx, cc):
        return (zz * 2 + yy, xx * 2 + cc)

    z_others = [z + 1 - 2 * (z % 2), (z + 2) % 4, 3 - z]
    z_dev = [device(zz, y, x, c) for zz in z_others]
    core_dev = device(z, y, x, 1 - c)
    x_dev = device(z, y, 1 - x, c)
    y_dev = device(z, 1 - y, x, c)
    far_dev = device(z, 1 - y, 1 - x, c)
    plane = [(3, far_dev), (2, x_dev), (1, y_dev)]

    barrier = pltpu.get_barrier_semaphore()
    partners = z_dev + [core_dev, x_dev, y_dev, far_dev]
    for partner in partners:
        pl.semaphore_signal(barrier, inc=1, device_id=partner, device_id_type=MESH)

    started = []

    def send(src, dst, to):
        n = len(started)
        copy = pltpu.make_async_remote_copy(
            src_ref=src,
            dst_ref=dst,
            send_sem=ssem.at[n],
            recv_sem=rsem.at[n],
            device_id=to,
            device_id_type=MESH,
        )
        copy.start()
        started.append(copy)
        return copy

    for copy in small:
        copy.wait()
    lane = lax.broadcasted_iota(jnp.int32, (steps, LANES), 1)
    diagonal = lax.broadcasted_iota(jnp.int32, (steps, steps), 0) == lax.broadcasted_iota(
        jnp.int32, (steps, steps), 1
    )
    slots = jnp.zeros(ids.shape, jnp.int32)
    for e in range(place.shape[1]):
        chosen = jnp.where(rep[...] == 0, place[0:1, e : e + 1], place[1:2, e : e + 1])
        slots = slots + jnp.where(ids[...] == e, chosen, 0)
    packed = jnp.zeros((steps, LANES), f32)
    for k in range(ids.shape[0]):
        slot = jnp.sum(jnp.where(diagonal, slots[k : k + 1], 0), axis=1, keepdims=True)
        gain = rw[k : k + 1].astype(f32)
        gain = jnp.sum(jnp.where(diagonal, gain, 0.0), axis=1, keepdims=True)
        packed = packed + jnp.where(lane == slot, gain, 0.0)
        packed = packed + jnp.where(lane == slot + 4, 1.0, 0.0)
    zbuf[0, :, width:] = packed.astype(bf16)
    for copy in own:
        copy.wait()
    pl.semaphore_wait(barrier, len(partners))

    z_in = [
        [
            send(zbuf.at[0, :, span(n)], zbuf.at[k + 1, :, span(n)], z_dev[k])
            for k in (2, 1, 0)
        ]
        for n in range(chunks)
    ]

    swapped = [
        send(w_gate_ref.at[0], wgu.at[:, pl.ds(2 * hid, hid)], core_dev),
        send(w_up_ref.at[0], wgu.at[:, pl.ds(3 * hid, hid)], core_dev),
        send(w_down_ref.at[0], wd.at[pl.ds(hid, hid)], core_dev),
    ]

    plane_in = {}

    def spread(n):
        for copy in z_in[n]:
            copy.wait_recv()
        lo, hi = edges[n], ends[n]
        gx[0, :, lo:hi] = jnp.concatenate([zbuf[k, :, lo:hi] for k in range(4)], axis=0)
        here = gx.at[0, :, span(n)]
        plane_in[n] = [send(here, gx.at[i, :, span(n)], to) for i, to in plane]

    def multiply(n, both):
        if n == 0:
            weights[0].wait()
            weights[1].wait()
            swapped[0].wait_recv()
            swapped[1].wait_recv()
        for copy in plane_in[n]:
            copy.wait_recv()
        lo, hi = edges[n], edges[n + 1]
        rows = gx[:, :, lo:hi].reshape(total, hi - lo)
        more = jnp.dot(rows, wgu[lo:hi], preferred_element_type=f32)
        return more if both is None else both + more

    both = None
    for n in range(chunks):
        spread(n)
    for n in range(chunks):
        both = multiply(n, both)

    hidden = []
    for i in range(2):
        gate, up = both[:, 2 * i * hid : (2 * i + 1) * hid], both[:, (2 * i + 1) * hid : (2 * i + 2) * hid]
        hidden.append((gate / (1.0 + jnp.exp(-gate)) * up).astype(bf16))
    hidden = jnp.concatenate(hidden, axis=1)
    route = gx[:, :, width : width + LANES].reshape(total, LANES).astype(f32)
    lane = lax.broadcasted_iota(jnp.int32, (total, LANES), 1)
    weight = jnp.sum(jnp.where(lane == z, route, 0.0), axis=1, keepdims=True)
    weights[2].wait()
    swapped[2].wait_recv()

    plane_out, z_out = {}, {}

    def down(n):
        lo, hi = edges[n], edges[n + 1]
        made = jnp.dot(hidden, wd[:, lo:hi], preferred_element_type=f32) * weight
        made = made.reshape(4, block, hi - lo)
        plane_out[n] = []
        for i, to in plane:
            qs[i - 1, :, lo:hi] = made[i].astype(bf16)
            here = qs.at[i - 1, :, columns(n)]
            plane_out[n].append(send(here, qr.at[i - 1, :, columns(n)], to))
        ps[:, lo:hi] = made[0]

    def across(n):
        lo, hi = edges[n], edges[n + 1]
        held = ps[:, lo:hi]
        for (i, _), copy in zip(reversed(plane), reversed(plane_out[n])):
            copy.wait_recv()
            held = held + qr[i - 1, :, lo:hi].astype(f32)
        held = held.astype(bf16)
        for k in range(4):
            tbuf[k, :, lo:hi] = held[k * steps : (k + 1) * steps]
        z_out[n] = [
            send(tbuf.at[k + 1, :, columns(n)], zr.at[k, :, columns(n)], z_dev[k])
            for k in (2, 1, 0)
        ]

    def finish(n):
        lo, hi = edges[n], edges[n + 1]
        final = tbuf[0, :, lo:hi].astype(f32)
        for copy in z_out[n]:
            copy.wait_recv()
        for k in range(3):
            final = final + zr[k, :, lo:hi].astype(f32)
        out_ref[:, lo:hi] = final.astype(out_ref.dtype)

    for n in range(chunks):
        down(n)
    counted = jnp.sum(jnp.where(lane == z + 4, route, 0.0), axis=1, keepdims=True)
    row = lax.broadcasted_iota(jnp.int32, (total, LANES), 0)
    per_step = jnp.where(lane == row % steps, counted, 0.0)
    per_step = jnp.sum(per_step, axis=0, keepdims=True)
    part_count[...] = jnp.broadcast_to(per_step, part_count.shape)
    count_in = send(part_count, other_count, core_dev)
    for n in range(chunks):
        across(n)
    count_in.wait_recv()
    count_ref[...] = (part_count[...] + other_count[...])[0:1, :steps].astype(jnp.int32)
    for n in range(chunks):
        finish(n)
    for copy in started:
        copy.wait_send()


def local_gathered(tokens, route_weight, expert_ids, replica, placement, w_gate, w_up, w_down):
    steps, own, width = tokens.shape
    hid = w_gate.shape[2]
    top = expert_ids.shape[2]
    cols = width // LANES
    tiles = [2 * cols // 7, cols - 2 * (2 * cols // 7), 2 * cols // 7]
    chunks = len(tiles)
    block = 4 * steps
    bf16, f32, i32 = jnp.bfloat16, jnp.float32, jnp.int32
    vmem = pl.BlockSpec(memory_space=pltpu.VMEM)
    anywhere = pl.BlockSpec(memory_space=pl.ANY)
    out, count = pl.pallas_call(
        functools.partial(moe_kernel, tiles),
        out_shape=(
            jax.ShapeDtypeStruct((steps, width), bf16),
            jax.ShapeDtypeStruct((1, steps), i32),
        ),
        in_specs=[anywhere] * 8,
        out_specs=(vmem, vmem),
        scratch_shapes=[
            pltpu.VMEM((top, steps), bf16),
            pltpu.VMEM((top, steps), i32),
            pltpu.VMEM((top, steps), i32),
            pltpu.VMEM((2, placement.shape[0]), i32),
            pltpu.VMEM((width, 4 * hid), bf16),
            pltpu.VMEM((2 * hid, width), bf16),
            pltpu.VMEM((4, steps, width + LANES), bf16),
            pltpu.VMEM((4, block, width + LANES), bf16),
            pltpu.VMEM((block, width), f32),
            pltpu.VMEM((3, block, width), bf16),
            pltpu.VMEM((3, block, width), bf16),
            pltpu.VMEM((4, steps, width), bf16),
            pltpu.VMEM((3, steps, width), bf16),
            pltpu.VMEM((8, LANES), f32),
            pltpu.VMEM((8, LANES), f32),
            pltpu.SemaphoreType.DMA((7 + chunks,)),
            pltpu.SemaphoreType.DMA((12 * chunks + 4,)),
            pltpu.SemaphoreType.DMA((12 * chunks + 4,)),
        ],
        compiler_params=pltpu.CompilerParams(
            collective_id=0, has_side_effects=True, vmem_limit_bytes=VMEM_LIMIT
        ),
    )(
        tokens.reshape(steps, width),
        route_weight.reshape(steps, top).T,
        expert_ids.reshape(steps, top).T,
        replica.reshape(steps, top).T,
        placement.T,
        w_gate,
        w_up,
        w_down,
    )
    return out.reshape(steps, own, width), count.reshape(steps, 1)


def solution(mesh):
    dense = mesh.shape["ep"] == 8 and mesh.shape["dp"] == 4
    return jax.shard_map(
        local_gathered if dense else local_packed,
        mesh=mesh,
        in_specs=(
            P(None, ("ep", "dp"), None),
            P(None, ("ep", "dp"), None),
            P(None, ("ep", "dp"), None),
            P(None, ("ep", "dp"), None),
            P(),
            P("ep", None, "dp"),
            P("ep", None, "dp"),
            P("ep", "dp", None),
        ),
        out_specs=(P(None, ("ep", "dp"), None), P(None, "ep")),
        check_vma=False,
    )
```

```python
import functools

import jax
import jax.numpy as jnp
from jax import lax
from jax.experimental import pallas as pl
from jax.experimental.pallas import tpu as pltpu
from jax.sharding import PartitionSpec as P

MESH = pl.DeviceIdType.MESH
LANES = 128
VMEM_LIMIT = 60 * 1024 * 1024


def pick_slots(expert_ids, replica, placement):
    logical = placement.shape[0]
    chosen = jnp.where(replica[..., None] == 0, placement[:, 0], placement[:, 1])
    matches = expert_ids[..., None] == jnp.arange(logical, dtype=jnp.int32)
    return jnp.sum(jnp.where(matches, chosen, 0), axis=-1)


def place_rows(group_slots, slot_count):
    flat_slots = group_slots.reshape(-1)
    matches = (flat_slots[:, None] == jnp.arange(slot_count, dtype=jnp.int32)[None, :]).astype(
        jnp.int32
    )
    earlier = jnp.cumsum(matches, axis=0) - matches
    position = jnp.sum(earlier * matches, axis=1)
    counts = jnp.sum(matches, axis=0)
    return (position.reshape(group_slots.shape), counts)


def pack_rows(rows, slots, slot_count, capacity, top_count):
    position, counts = place_rows(slots, slot_count)
    target = (slots * capacity + position).reshape(-1)
    repeated = jnp.repeat(rows, top_count, axis=0)
    packed = jnp.zeros((slot_count * capacity, rows.shape[1]), rows.dtype).at[target].set(repeated)
    return (packed.reshape(slot_count, capacity, rows.shape[1]), target)


def expert_block(expert_rows, w_gate, w_up, w_down):
    gate_out = jnp.dot(expert_rows, w_gate[0], preferred_element_type=jnp.float32)
    up_out = jnp.dot(expert_rows, w_up[0], preferred_element_type=jnp.float32)
    hidden = (jax.nn.silu(gate_out) * up_out).astype(jnp.bfloat16)
    return jnp.dot(hidden, w_down[0], preferred_element_type=jnp.float32).astype(jnp.bfloat16)


def combine_rows(
    returned, target, weight_rows, row_count, top_count, slot_count, capacity, model_width
):
    paired = returned.reshape(slot_count, 2, capacity, model_width)
    first_half = paired[:, 0].reshape(-1, model_width)[target].astype(jnp.float32)
    second_half = paired[:, 1].reshape(-1, model_width)[target].astype(jnp.float32)
    weighted = (first_half + second_half) * weight_rows.reshape(-1, 1).astype(jnp.float32)
    return jnp.sum(weighted.reshape(row_count, top_count, model_width), axis=1)


def local_packed(tokens, route_weight, expert_ids, replica, placement, w_gate, w_up, w_down):
    steps_total = tokens.shape[0]
    model_width = tokens.shape[2]
    ep_count = lax.axis_size("ep")
    dp_count = lax.axis_size("dp")
    slot_count = ep_count // 2
    logical = placement.shape[0]
    top_count = expert_ids.shape[2]
    own_count = expert_ids.shape[1]
    group_size = own_count * dp_count
    capacity = 2 * ((group_size * top_count + logical) // (2 * logical)) + 2
    own_slots = pick_slots(expert_ids, replica, placement)
    outputs = []
    load_rows = []
    for step_index in range(steps_total):
        group_slots = lax.all_gather(own_slots[step_index], "dp", axis=0, tiled=True)
        group_counts = place_rows(group_slots, slot_count)[1]
        arrived_counts = lax.all_to_all(
            jnp.repeat(group_counts, 2), "ep", split_axis=0, concat_axis=0, tiled=True
        )
        grouped, group_weight = (
            lax.all_gather(tokens[step_index], "dp", axis=0, tiled=True),
            lax.all_gather(route_weight[step_index], "dp", axis=0, tiled=True),
        )
        send_rows, target = pack_rows(grouped, group_slots, slot_count, capacity, top_count)
        arrived = lax.all_to_all(
            jnp.repeat(send_rows, 2, axis=0), "ep", split_axis=0, concat_axis=0, tiled=True
        )
        block_out = expert_block(arrived.reshape(-1, model_width), w_gate, w_up, w_down)
        returned = lax.all_to_all(
            block_out.reshape(ep_count, capacity, model_width),
            "ep",
            split_axis=0,
            concat_axis=0,
            tiled=True,
        )
        partial_tokens = combine_rows(
            returned, target, group_weight, group_size, top_count, slot_count, capacity, model_width
        )
        token_out = lax.psum_scatter(partial_tokens, "dp", scatter_dimension=0, tiled=True)
        outputs.append(token_out.astype(jnp.bfloat16))
        load_rows.append(jnp.sum(arrived_counts).reshape(1))
    return (jnp.stack(outputs), jnp.stack(load_rows))


def moe_kernel(
    tiles,
    tok_ref,
    rw_ref,
    ids_ref,
    rep_ref,
    place_ref,
    w_gate_ref,
    w_up_ref,
    w_down_ref,
    out_ref,
    count_ref,
    rw,
    ids,
    rep,
    place,
    wgu,
    wd,
    zbuf,
    gx,
    ps,
    qs,
    qr,
    tbuf,
    zr,
    part_count,
    other_count,
    wsem,
    ssem,
    rsem,
):
    ep, dp = lax.axis_index("ep"), lax.axis_index("dp")
    z, y = ep // 2, ep % 2
    x, c = dp // 2, dp % 2
    steps, width = tok_ref.shape
    hid = w_gate_ref.shape[2]
    chunks = len(tiles)
    edges = [sum(tiles[:n]) * LANES for n in range(chunks + 1)]
    ends = edges[1:chunks] + [width + LANES]
    block = 4 * steps
    total = 4 * block
    f32, bf16 = jnp.float32, jnp.bfloat16

    def columns(n):
        return pl.ds(edges[n], edges[n + 1] - edges[n])

    def span(n):
        return pl.ds(edges[n], ends[n] - edges[n])

    def load(src, dst, n):
        copy = pltpu.make_async_copy(src, dst, wsem.at[n])
        copy.start()
        return copy

    small = [
        load(src, dst, n)
        for n, (src, dst) in enumerate(
            [(rw_ref, rw), (ids_ref, ids), (rep_ref, rep), (place_ref, place)]
        )
    ]
    own = [
        load(tok_ref.at[:, columns(n)], zbuf.at[0, :, columns(n)], 4 + n)
        for n in range(chunks)
    ]
    weights = [
        load(w_gate_ref.at[0], wgu.at[:, pl.ds(0, hid)], 4 + chunks),
        load(w_up_ref.at[0], wgu.at[:, pl.ds(hid, hid)], 5 + chunks),
        load(w_down_ref.at[0], wd.at[pl.ds(0, hid)], 6 + chunks),
    ]

    def device(zz, yy, xx, cc):
        return (zz * 2 + yy, xx * 2 + cc)

    z_others = [z + 1 - 2 * (z % 2), (z + 2) % 4, 3 - z]
    z_dev = [device(zz, y, x, c) for zz in z_others]
    core_dev = device(z, y, x, 1 - c)
    x_dev = device(z, y, 1 - x, c)
    y_dev = device(z, 1 - y, x, c)
    far_dev = device(z, 1 - y, 1 - x, c)
    plane = [(1, y_dev), (3, far_dev), (2, x_dev)]

    barrier = pltpu.get_barrier_semaphore()
    partners = z_dev + [core_dev, x_dev, y_dev, far_dev]
    for partner in partners:
        pl.semaphore_signal(barrier, inc=1, device_id=partner, device_id_type=MESH)

    started = []

    def send(src, dst, to):
        n = len(started)
        copy = pltpu.make_async_remote_copy(
            src_ref=src,
            dst_ref=dst,
            send_sem=ssem.at[n],
            recv_sem=rsem.at[n],
            device_id=to,
            device_id_type=MESH,
        )
        copy.start()
        started.append(copy)
        return copy

    for copy in small:
        copy.wait()
    lane = lax.broadcasted_iota(jnp.int32, (steps, LANES), 1)
    diagonal = lax.broadcasted_iota(jnp.int32, (steps, steps), 0) == lax.broadcasted_iota(
        jnp.int32, (steps, steps), 1
    )
    slots = jnp.zeros(ids.shape, jnp.int32)
    for e in range(place.shape[1]):
        chosen = jnp.where(rep[...] == 0, place[0:1, e : e + 1], place[1:2, e : e + 1])
        slots = slots + jnp.where(ids[...] == e, chosen, 0)
    packed = jnp.zeros((steps, LANES), f32)
    for k in range(ids.shape[0]):
        slot = jnp.sum(jnp.where(diagonal, slots[k : k + 1], 0), axis=1, keepdims=True)
        gain = rw[k : k + 1].astype(f32)
        gain = jnp.sum(jnp.where(diagonal, gain, 0.0), axis=1, keepdims=True)
        packed = packed + jnp.where(lane == slot, gain, 0.0)
        packed = packed + jnp.where(lane == slot + 4, 1.0, 0.0)
    zbuf[0, :, width:] = packed.astype(bf16)
    for copy in own:
        copy.wait()
    pl.semaphore_wait(barrier, len(partners))

    z_in = [
        [
            send(zbuf.at[0, :, span(n)], zbuf.at[k + 1, :, span(n)], z_dev[k])
            for k in (2, 1, 0)
        ]
        for n in range(chunks)
    ]

    swapped = [
        send(w_gate_ref.at[0], wgu.at[:, pl.ds(2 * hid, hid)], core_dev),
        send(w_up_ref.at[0], wgu.at[:, pl.ds(3 * hid, hid)], core_dev),
        send(w_down_ref.at[0], wd.at[pl.ds(hid, hid)], core_dev),
    ]

    plane_in = {}

    def spread(n):
        for copy in z_in[n]:
            copy.wait_recv()
        lo, hi = edges[n], ends[n]
        gx[0, :, lo:hi] = jnp.concatenate([zbuf[k, :, lo:hi] for k in range(4)], axis=0)
        here = gx.at[0, :, span(n)]
        plane_in[n] = [send(here, gx.at[i, :, span(n)], to) for i, to in plane]

    def multiply(n, both):
        if n == 0:
            weights[0].wait()
            weights[1].wait()
            swapped[0].wait_recv()
            swapped[1].wait_recv()
        for copy in plane_in[n]:
            copy.wait_recv()
        lo, hi = edges[n], edges[n + 1]
        rows = gx[:, :, lo:hi].reshape(total, hi - lo)
        more = jnp.dot(rows, wgu[lo:hi], preferred_element_type=f32)
        return more if both is None else both + more

    both = None
    for n in range(chunks):
        spread(n)
    for n in range(chunks):
        both = multiply(n, both)

    hidden = []
    for i in range(2):
        gate, up = both[:, 2 * i * hid : (2 * i + 1) * hid], both[:, (2 * i + 1) * hid : (2 * i + 2) * hid]
        hidden.append((gate / (1.0 + jnp.exp(-gate)) * up).astype(bf16))
    hidden = jnp.concatenate(hidden, axis=1)
    route = gx[:, :, width : width + LANES].reshape(total, LANES).astype(f32)
    lane = lax.broadcasted_iota(jnp.int32, (total, LANES), 1)
    weight = jnp.sum(jnp.where(lane == z, route, 0.0), axis=1, keepdims=True)
    weights[2].wait()
    swapped[2].wait_recv()

    plane_out, z_out = {}, {}

    def down(n):
        lo, hi = edges[n], edges[n + 1]
        made = jnp.dot(hidden, wd[:, lo:hi], preferred_element_type=f32) * weight
        made = made.reshape(4, block, hi - lo)
        plane_out[n] = []
        for i, to in plane:
            qs[i - 1, :, lo:hi] = made[i].astype(bf16)
            here = qs.at[i - 1, :, columns(n)]
            plane_out[n].append(send(here, qr.at[i - 1, :, columns(n)], to))
        ps[:, lo:hi] = made[0]

    def across(n):
        lo, hi = edges[n], edges[n + 1]
        held = ps[:, lo:hi]
        for (i, _), copy in zip(reversed(plane), reversed(plane_out[n])):
            copy.wait_recv()
            held = held + qr[i - 1, :, lo:hi].astype(f32)
        held = held.astype(bf16)
        for k in range(4):
            tbuf[k, :, lo:hi] = held[k * steps : (k + 1) * steps]
        z_out[n] = [
            send(tbuf.at[k + 1, :, columns(n)], zr.at[k, :, columns(n)], z_dev[k])
            for k in (2, 1, 0)
        ]

    def finish(n):
        lo, hi = edges[n], edges[n + 1]
        final = tbuf[0, :, lo:hi].astype(f32)
        for copy in z_out[n]:
            copy.wait_recv()
        for k in range(3):
            final = final + zr[k, :, lo:hi].astype(f32)
        out_ref[:, lo:hi] = final.astype(out_ref.dtype)

    for n in range(chunks):
        down(n)
    counted = jnp.sum(jnp.where(lane == z + 4, route, 0.0), axis=1, keepdims=True)
    row = lax.broadcasted_iota(jnp.int32, (total, LANES), 0)
    per_step = jnp.where(lane == row % steps, counted, 0.0)
    per_step = jnp.sum(per_step, axis=0, keepdims=True)
    part_count[...] = jnp.broadcast_to(per_step, part_count.shape)
    count_in = send(part_count, other_count, core_dev)
    for n in range(chunks):
        across(n)
    count_in.wait_recv()
    count_ref[...] = (part_count[...] + other_count[...])[0:1, :steps].astype(jnp.int32)
    for n in range(chunks):
        finish(n)
    for copy in started:
        copy.wait_send()


def local_gathered(tokens, route_weight, expert_ids, replica, placement, w_gate, w_up, w_down):
    steps, own, width = tokens.shape
    hid = w_gate.shape[2]
    top = expert_ids.shape[2]
    cols = width // LANES
    tiles = [2 * cols // 7, cols - 2 * (2 * cols // 7), 2 * cols // 7]
    chunks = len(tiles)
    block = 4 * steps
    bf16, f32, i32 = jnp.bfloat16, jnp.float32, jnp.int32
    vmem = pl.BlockSpec(memory_space=pltpu.VMEM)
    anywhere = pl.BlockSpec(memory_space=pl.ANY)
    out, count = pl.pallas_call(
        functools.partial(moe_kernel, tiles),
        out_shape=(
            jax.ShapeDtypeStruct((steps, width), bf16),
            jax.ShapeDtypeStruct((1, steps), i32),
        ),
        in_specs=[anywhere] * 8,
        out_specs=(vmem, vmem),
        scratch_shapes=[
            pltpu.VMEM((top, steps), bf16),
            pltpu.VMEM((top, steps), i32),
            pltpu.VMEM((top, steps), i32),
            pltpu.VMEM((2, placement.shape[0]), i32),
            pltpu.VMEM((width, 4 * hid), bf16),
            pltpu.VMEM((2 * hid, width), bf16),
            pltpu.VMEM((4, steps, width + LANES), bf16),
            pltpu.VMEM((4, block, width + LANES), bf16),
            pltpu.VMEM((block, width), f32),
            pltpu.VMEM((3, block, width), bf16),
            pltpu.VMEM((3, block, width), bf16),
            pltpu.VMEM((4, steps, width), bf16),
            pltpu.VMEM((3, steps, width), bf16),
            pltpu.VMEM((8, LANES), f32),
            pltpu.VMEM((8, LANES), f32),
            pltpu.SemaphoreType.DMA((7 + chunks,)),
            pltpu.SemaphoreType.DMA((12 * chunks + 4,)),
            pltpu.SemaphoreType.DMA((12 * chunks + 4,)),
        ],
        compiler_params=pltpu.CompilerParams(
            collective_id=0, has_side_effects=True, vmem_limit_bytes=VMEM_LIMIT
        ),
    )(
        tokens.reshape(steps, width),
        route_weight.reshape(steps, top).T,
        expert_ids.reshape(steps, top).T,
        replica.reshape(steps, top).T,
        placement.T,
        w_gate,
        w_up,
        w_down,
    )
    return out.reshape(steps, own, width), count.reshape(steps, 1)


def solution(mesh):
    dense = mesh.shape["ep"] == 8 and mesh.shape["dp"] == 4
    return jax.shard_map(
        local_gathered if dense else local_packed,
        mesh=mesh,
        in_specs=(
            P(None, ("ep", "dp"), None),
            P(None, ("ep", "dp"), None),
            P(None, ("ep", "dp"), None),
            P(None, ("ep", "dp"), None),
            P(),
            P("ep", None, "dp"),
            P("ep", None, "dp"),
            P("ep", "dp", None),
        ),
        out_specs=(P(None, ("ep", "dp"), None), P(None, "ep")),
        check_vma=False,
    )
```
